128 devices in a mesh: dp: 16 (over y, z), tensor: 8 (over x, core).
Axes of the slice: x: 4, y: 4, z: 4, core: 2. Of those that a mesh axis runs over, the one named last changes fastest.
Arguments:
- grad: bfloat16 [16, 2, 3072, 5120], P('dp', None, 'tensor'), may hold values from -32 to 32
- error: bfloat16 [16, 2, 3072, 5120], P('dp', None, 'tensor'), may hold values from -4 to 4
- q_init: bfloat16 [5120, 2, 32], replicated, may hold values from -6 to 6
Outputs:
- new_error: bfloat16 [16, 2, 3072, 5120], P('dp', None, 'tensor')
- p_factor: float32 [2, 3072, 32], P(None, 'tensor')
- q_factor: float32 [5120, 2, 32], P(('dp', 'tensor'))
The draws below stay inside these ranges and needn't reach their ends.
All inputs are finite; a program needn't handle non-finite values.
Results may differ from the reference program's by a relative error of at most 0.018.
Values may be sent and summed in bfloat16 or wider, within the bound.
No kernel may reach another device: no remote copies, remote signals or barrier semaphores. Data moves between devices by JAX's collectives and lax.ppermute only.
A program may use at most 128 MiB of HBM per device.

```python
import math
import jax
import jax.numpy as jnp
from jax import lax

D = 5120
RANK = 32
MATS = 2
ROWS = 3072
REPLICAS = 16
N_DP = 16


def draw_grad(key, part):
    key = jax.random.fold_in(key, 11)
    subkeys = jax.random.split(key, 6)
    common_rank = RANK + RANK // 2
    full_shape = (REPLICAS, MATS, ROWS, D)
    noise_part = jax.random.normal(subkeys[0], full_shape, jnp.float32)
    left_factor = jax.random.normal(subkeys[1], (MATS, ROWS, common_rank), jnp.float32)
    right_factor = jax.random.normal(subkeys[2], (MATS, D, common_rank), jnp.float32)
    mixing = jax.random.uniform(subkeys[4], (REPLICAS, MATS, 1, common_rank), jnp.float32, 0.4, 1.6)
    pairing = jax.random.permutation(subkeys[5], REPLICAS).astype(jnp.int32)
    column_block = jnp.arange(D, dtype=jnp.int32) // (D // REPLICAS)
    spike_scale = jnp.where(column_block[None, :] == pairing[:, None], 14.0, 1.0).astype(jnp.float32)
    common_part = jnp.einsum('rmik,mjk->rmij', left_factor[None] * mixing, right_factor, precision=lax.Precision.HIGHEST) * (1.4 / math.sqrt(common_rank))
    combined = noise_part * spike_scale[:, None, None, :] + common_part
    return jnp.clip(combined, -32.0, 32.0).astype(jnp.bfloat16)


def block_levels(rng, dims, pieces, smallest, top_value):
    def one(dim, blocks):
        draws = jax.random.uniform(jax.random.fold_in(jax.random.fold_in(rng, 6), dim), (blocks,), jnp.float32, smallest / len(pieces), top_value / len(pieces))
        return jnp.repeat(jnp.exp(draws), dims[dim] // blocks).reshape((-1,) + (1,) * (len(dims) - dim - 1))

    loudness = one(*pieces[0])
    for cut in pieces[1:]:
        loudness = loudness * one(*cut)
    return loudness


def scatter_about(own_key, dims, deviation, bound, cuts=(), kind=jnp.bfloat16):
    result = deviation * jax.random.normal(own_key, dims, jnp.float32)
    if cuts:
        result = result * block_levels(own_key, dims, cuts, -0.22, 0.18)
    return jnp.clip(result, -bound, bound).astype(kind)


def setup_inputs(seed: int = 0) -> dict:
    key_list = jax.random.split(jax.random.key(seed), 4)
    return {
        "grad": draw_grad(jax.random.fold_in(key_list[3], 71), 0),
        "error": scatter_about(key_list[1], (REPLICAS, MATS, ROWS, D), 0.5, 4.0, ((0, 16), (2, 8))),
        "q_init": scatter_about(key_list[2], (D, MATS, RANK), 1.0, 6.0),
    }


def inverse_factor(gram):
    rank_width = gram.shape[-1]
    identity = jnp.eye(rank_width, dtype=jnp.float32)
    trace_sum = jnp.trace(gram, axis1=1, axis2=2)
    shifted = gram + (1e-05 * trace_sum / rank_width)[:, None, None] * identity
    factor = jnp.linalg.cholesky(shifted)
    return jax.vmap(lambda single: jax.scipy.linalg.solve_triangular(single, identity, lower=True))(factor)

def reference(grad, error, q_init):
    p_blocks = []
    q_blocks = []
    error_blocks = []
    for matrix in range(MATS):
        corrected = [(grad[replica, matrix].astype(jnp.float32) + error[replica, matrix].astype(jnp.float32)).astype(jnp.bfloat16) for replica in range(N_DP)]
        q_start = q_init[:, matrix, :]
        summed = jnp.zeros((ROWS, RANK), jnp.float32)
        for replica in range(N_DP):
            summed = summed + jnp.dot(corrected[replica].astype(jnp.float32), q_start.astype(jnp.float32), preferred_element_type=jnp.float32)
        gram_full = jnp.dot(summed.T, summed, precision=lax.Precision.HIGHEST)
        inverse = inverse_factor(gram_full[None])[0]
        p_fac = jnp.dot(summed, inverse.T, precision=lax.Precision.HIGHEST)
        p_round = summed.astype(jnp.bfloat16)
        projected = jnp.zeros((D, RANK), jnp.float32)
        for replica in range(N_DP):
            projected = projected + jnp.dot(corrected[replica].T.astype(jnp.float32), p_round.astype(jnp.float32), preferred_element_type=jnp.float32)
        q_fac = jnp.dot(projected, inverse.T, precision=lax.Precision.HIGHEST) / N_DP
        rebuilt = jnp.dot(p_fac.astype(jnp.bfloat16).astype(jnp.float32), q_fac.astype(jnp.bfloat16).T.astype(jnp.float32), preferred_element_type=jnp.float32)
        error_blocks.append(jnp.stack([(corrected[replica].astype(jnp.float32) - rebuilt).astype(jnp.bfloat16) for replica in range(N_DP)], axis=0))
        p_blocks.append(p_fac)
        q_blocks.append(q_fac)
    return (jnp.stack(error_blocks, axis=1), jnp.stack(p_blocks, axis=0), jnp.stack(q_blocks, axis=1))
```

```python
import jax
import jax.numpy as jnp
from jax import lax
from jax.experimental import pallas as pl
from jax.experimental.pallas import tpu as pltpu
from jax.sharding import PartitionSpec as P

F32 = jnp.float32
BF16 = jnp.bfloat16
HIGHEST = lax.Precision.HIGHEST
NN = (((1,), (0,)), ((), ()))
NT = (((1,), (1,)), ((), ()))
VMEM_BYTES = 32 * 1024 * 1024

MATS, ROWS, WIDTH, RANK = 2, 384, 5120, 32
BOTH = MATS * RANK
HALF = WIDTH // 2
LANES = 2 * BOTH
DP, TENSOR = 16, 8
DEVICES = DP * TENSOR
HEAD = 16 * DEVICES
CHUNK = 24
FIRST_STEP = 512
LAST_STEP = 512


def left_kernel(grad_ref, error_ref, q_ref, corrected_ref, out_ref, acc_ref):
    step = pl.program_id(0)

    @pl.when(step == 0)
    def _():
        acc_ref[...] = jnp.zeros_like(acc_ref)

    columns = pl.ds(pl.multiple_of(step * FIRST_STEP, FIRST_STEP), FIRST_STEP)
    for m in range(MATS):
        corrected = (grad_ref[m].astype(F32) + error_ref[m].astype(F32)).astype(BF16)
        corrected_ref[m, :, columns] = corrected
        acc_ref[m] += lax.dot_general(corrected, q_ref[m], NT, preferred_element_type=F32)

    @pl.when(step == pl.num_programs(0) - 1)
    def _():
        part = jnp.concatenate([acc_ref[m].T for m in range(MATS)], axis=0).astype(BF16)
        for r in range(DP):
            out_ref[r] = part


def right_kernel(parts_ref, corrected_ref, out_ref, summed_ref, turned_ref, tail_ref, gram_ref):
    summed = parts_ref[0].astype(F32)
    for r in range(1, DP):
        summed = summed + parts_ref[r].astype(F32)
    summed_ref[...] = summed
    left = [summed[m * RANK : (m + 1) * RANK] for m in range(MATS)]
    left_round = [x.astype(BF16) for x in left]

    gram = jnp.concatenate(
        [lax.dot_general(x, x, NT, precision=HIGHEST, preferred_element_type=F32) for x in left], axis=0
    )
    gram_ref[...] = jnp.concatenate([gram[16 * a : 16 * a + 16] for a in range(4)], axis=1)
    row = gram_ref[pl.ds(lax.axis_index("dp"), 1), :]
    high = row.astype(BF16).astype(F32)
    middle = (row - high).astype(BF16).astype(F32)
    low = row - high - middle
    terms = jnp.concatenate([high, middle, low, jnp.zeros_like(row)], axis=0)

    def columns_step(i, carry):
        products = []
        for h in range(2):
            columns = pl.ds(pl.multiple_of(HALF * h + 256 * i, 256), 256)
            for m in range(MATS):
                products.append(
                    lax.dot_general(left_round[m], corrected_ref[m, :, columns], NN, preferred_element_type=F32)
                )
        turned_ref[pl.ds(pl.multiple_of(256 * i, 256), 256), :] = jnp.concatenate(products, axis=0).T
        return carry

    lax.fori_loop(0, HALF // 256, columns_step, 0, unroll=2)

    for c in range(DEVICES):
        tail_ref[c, 0:4, :] = turned_ref[HEAD + 4 * c : HEAD + 4 * c + 4, :]
    tail_ref[:, 4:8, :] = jnp.broadcast_to(terms[None], (DEVICES, 4, LANES))
    for g in range(DEVICES // 16):
        head = turned_ref[256 * g : 256 * g + 256, :].reshape(16, 16, LANES)
        out_ref[16 * g : 16 * g + 16] = jnp.concatenate(
            [head, tail_ref[16 * g : 16 * g + 16]], axis=1
        ).astype(BF16)


def inverse_factors(grams):
    row = lax.broadcasted_iota(jnp.int32, (RANK, LANES), 0)
    lane = lax.broadcasted_iota(jnp.int32, (RANK, LANES), 1)
    first = (lane // RANK) % 2 == 0
    eye = (lane % RANK == row).astype(F32)
    square = jnp.concatenate(list(grams) + [jnp.zeros((RANK, LANES - BOTH), F32)], axis=1)
    diagonal = square * eye
    trace = [
        jnp.sum(jnp.where(lane // RANK == m, diagonal, 0.0), axis=(0, 1), keepdims=True) for m in range(MATS)
    ]
    shift = 1e-05 * jnp.where(first, trace[0], trace[1]) / RANK
    work = square + jnp.where(lane < BOTH, shift * eye, eye)
    for j in range(RANK - 1):
        column = jnp.where(first, work[:, j : j + 1], work[:, RANK + j : RANK + j + 1])
        pivot_row = work[j : j + 1, :]
        scaled = pivot_row / column[j : j + 1, :]
        work = work - jnp.where(row > j, column, 0.0) * scaled
    pivots = work * eye
    pivot = [
        jnp.sum(jnp.where(lane // RANK == m, pivots, 0.0), axis=1, keepdims=True) for m in range(MATS)
    ]
    return work / jnp.sqrt(jnp.where(first, pivot[0], pivot[1]))


def factor_kernel(parts_ref, summed_ref, out_ref, p_ref, gram_ref):
    total = jnp.zeros((CHUNK, LANES), F32)
    for r in range(DP):
        block = parts_ref[TENSOR * r].astype(F32)
        for t in range(1, TENSOR):
            block = block + parts_ref[TENSOR * r + t].astype(F32)
        total = total + block
        gram_ref[r : r + 1, :] = block[20:21] + block[21:22] + block[22:23]
    gram = gram_ref[...]
    gram = jnp.concatenate([gram[:, RANK * a : RANK * a + RANK] for a in range(4)], axis=0)
    inverse = inverse_factors([gram[m * RANK : (m + 1) * RANK] for m in range(MATS)])

    lane = lax.broadcasted_iota(jnp.int32, (RANK, LANES), 1)
    turned = pltpu.roll(inverse, BOTH, 1)
    weights = jnp.concatenate(
        [
            jnp.where(lane // RANK == 2 * h + m, inverse if h else turned, 0.0)
            for h in range(2)
            for m in range(MATS)
        ],
        axis=0,
    )
    right = lax.dot_general(total, weights, NT, precision=HIGHEST, preferred_element_type=F32) / DP
    row = lax.broadcasted_iota(jnp.int32, (CHUNK, LANES), 0)
    right = jnp.where(row < 20, right, 0.0).astype(BF16)
    out_ref[...] = jnp.broadcast_to(right[None], (DEVICES, CHUNK, LANES))
    p_ref[...] = lax.dot_general(
        weights[:BOTH, :BOTH], summed_ref[...], NN, precision=HIGHEST, preferred_element_type=F32
    )


def error_kernel(right_ref, p_ref, corrected_ref, out_ref, q_ref, wide_ref, turned_ref, left_ref):
    step = pl.program_id(0)

    @pl.when(step == 0)
    def _():
        for g in range(DEVICES // 16):
            block = right_ref[16 * g : 16 * g + 16].astype(F32)
            wide_ref[256 * g : 256 * g + 256, :] = block[:, 0:16].reshape(256, LANES)
            for c in range(16):
                start = HEAD + 4 * (16 * g + c)
                wide_ref[start : start + 4, :] = block[c, 16:20]
        wide_ref[HALF:, :] = jnp.zeros((LANES, LANES), F32)
        turned_ref[...] = wide_ref[:HALF, :].astype(BF16)
        p = p_ref[...].T
        p = jnp.concatenate([p, p], axis=1)
        lane = lax.broadcasted_iota(jnp.int32, (ROWS, LANES), 1)
        for h in range(2):
            for m in range(MATS):
                left_ref[h, ROWS * m : ROWS * m + ROWS, :] = jnp.where(
                    lane // RANK == 2 * h + m, p, 0.0
                ).astype(BF16)
        me = lax.axis_index(("dp", "tensor"))
        share = WIDTH // DEVICES
        start = pl.multiple_of(share * (me % (DEVICES // 2)), 8)
        own = wide_ref[pl.ds(start, LANES), :].T
        q_ref[...] = jnp.where(me < DEVICES // 2, own[:BOTH, :share], own[BOTH:, :share])

    per_half = HALF // LAST_STEP
    h = step // per_half
    rows = pl.ds(pl.multiple_of((step % per_half) * LAST_STEP, LAST_STEP), LAST_STEP)
    columns = pl.ds(pl.multiple_of(step * LAST_STEP, LAST_STEP), LAST_STEP)
    rebuilt = lax.dot_general(left_ref[h], turned_ref[rows, :], NT, preferred_element_type=F32)
    for m in range(MATS):
        out_ref[m] = (
            corrected_ref[m, :, columns].astype(F32) - rebuilt[ROWS * m : ROWS * m + ROWS]
        ).astype(BF16)


def params(grid=True):
    return pltpu.CompilerParams(
        dimension_semantics=("arbitrary",) if grid else None, vmem_limit_bytes=VMEM_BYTES
    )


WHOLE = pl.BlockSpec(memory_space=pltpu.VMEM)


def local(grad, error, q_init):
    q_turned = q_init.transpose(1, 2, 0)
    step_spec = pl.BlockSpec((MATS, ROWS, FIRST_STEP), lambda i: (0, 0, i))
    corrected, part = pl.pallas_call(
        left_kernel,
        grid=(WIDTH // FIRST_STEP,),
        in_specs=[step_spec, step_spec, pl.BlockSpec((MATS, RANK, FIRST_STEP), lambda i: (0, 0, i))],
        out_specs=[WHOLE, WHOLE],
        out_shape=[
            pltpu.VMEM((MATS, ROWS, WIDTH), BF16),
            jax.ShapeDtypeStruct((DP, BOTH, ROWS), BF16),
        ],
        scratch_shapes=[pltpu.VMEM((MATS, ROWS, RANK), F32)],
        compiler_params=params(),
        name="left_product",
    )(grad[0], error[0], q_turned)

    parts = lax.all_to_all(part, "dp", 0, 0, tiled=True)

    partial_q, summed = pl.pallas_call(
        right_kernel,
        in_specs=[WHOLE, WHOLE],
        out_specs=[WHOLE, WHOLE],
        out_shape=[
            jax.ShapeDtypeStruct((DEVICES, CHUNK, LANES), BF16),
            jax.ShapeDtypeStruct((BOTH, ROWS), F32),
        ],
        scratch_shapes=[
            pltpu.VMEM((HALF, LANES), F32),
            pltpu.VMEM((DEVICES, 8, LANES), F32),
            pltpu.VMEM((16, LANES), F32),
        ],
        compiler_params=params(False),
        name="right_product",
    )(parts, corrected)

    partial_q = lax.all_to_all(partial_q, ("dp", "tensor"), 0, 0, tiled=True)

    q_own, p_turned = pl.pallas_call(
        factor_kernel,
        in_specs=[WHOLE, WHOLE],
        out_specs=[WHOLE, WHOLE],
        out_shape=[
            jax.ShapeDtypeStruct((DEVICES, CHUNK, LANES), BF16),
            jax.ShapeDtypeStruct((BOTH, ROWS), F32),
        ],
        scratch_shapes=[pltpu.VMEM((16, LANES), F32)],
        compiler_params=params(False),
        name="factor",
    )(partial_q, summed)

    q_all = lax.all_to_all(q_own, ("dp", "tensor"), 0, 0, tiled=True)

    new_error, q_factor = pl.pallas_call(
        error_kernel,
        grid=(WIDTH // LAST_STEP,),
        in_specs=[WHOLE, WHOLE, WHOLE],
        out_specs=[pl.BlockSpec((MATS, ROWS, LAST_STEP), lambda i: (0, 0, i)), WHOLE],
        out_shape=[
            jax.ShapeDtypeStruct((MATS, ROWS, WIDTH), BF16),
            jax.ShapeDtypeStruct((BOTH, WIDTH // DEVICES), F32),
        ],
        scratch_shapes=[
            pltpu.VMEM((HALF + LANES, LANES), F32),
            pltpu.VMEM((HALF, LANES), BF16),
            pltpu.VMEM((2, MATS * ROWS, LANES), BF16),
        ],
        compiler_params=params(),
        name="new_error",
    )(q_all, p_turned, corrected)

    return (
        new_error[None],
        p_turned.reshape(MATS, RANK, ROWS).transpose(0, 2, 1),
        q_factor.reshape(MATS, RANK, WIDTH // DEVICES).transpose(2, 0, 1),
    )


def solution(mesh):
    in_specs = (P("dp", None, "tensor", None), P("dp", None, "tensor", None), P())
    out_specs = (
        P("dp", None, "tensor", None),
        P(None, "tensor", None),
        P(("dp", "tensor"), None, None),
    )
    return jax.shard_map(local, mesh=mesh, in_specs=in_specs, out_specs=out_specs, check_vma=False)
```

```python
import jax
import jax.numpy as jnp
from jax import lax
from jax.experimental import pallas as pl
from jax.experimental.pallas import tpu as pltpu
from jax.sharding import PartitionSpec as P

F32 = jnp.float32
BF16 = jnp.bfloat16
HIGHEST = lax.Precision.HIGHEST
NN = (((1,), (0,)), ((), ()))
NT = (((1,), (1,)), ((), ()))
VMEM_BYTES = 36 * 1024 * 1024

MATS, ROWS, WIDTH, RANK = 2, 384, 5120, 32
BOTH = MATS * RANK
HALF, QUARTER = WIDTH // 2, WIDTH // 4
LANES = 2 * BOTH
DP, TENSOR = 16, 8
DEVICES = DP * TENSOR
CHIPS = DEVICES // 2
CHIPS_X = TENSOR // 2
SHARE = WIDTH // DEVICES
HEAD = 16 * CHIPS
CHUNK = 24
STEP = 512
TILE = 256
BOTH_AXES = ("dp", "tensor")
CORE_PAIRS = [(i, i ^ 1) for i in range(TENSOR)]
SAME_CORE = [[i for i in range(DEVICES) if i % 2 == core] for core in range(2)]


def columns_at(start, size):
    return pl.ds(pl.multiple_of(start, TILE), size)


def left_kernel(grad_ref, error_ref, q_ref, corrected_ref, out_ref, error_vmem, q_vmem, acc_ref, sems):
    starts = range(0, WIDTH, STEP)
    copies = []
    for i, start in enumerate(starts):
        columns = pl.ds(start, STEP)
        pairs = [(q_ref, q_vmem), (grad_ref, corrected_ref), (error_ref, error_vmem)]
        copies.append(
            [
                pltpu.make_async_copy(source.at[:, :, columns], target.at[:, :, columns], sems.at[n, i])
                for n, (source, target) in enumerate(pairs)
            ]
        )
        for copy in copies[-1]:
            copy.start()
    for i, start in enumerate(starts):
        columns = pl.ds(start, STEP)
        for copy in copies[i]:
            copy.wait()
        for m in range(MATS):
            corrected = (corrected_ref[m, :, columns].astype(F32) + error_vmem[m, :, columns].astype(F32)).astype(BF16)
            corrected_ref[m, :, columns] = corrected
            product = lax.dot_general(corrected, q_vmem[m, :, columns], NT, preferred_element_type=F32)
            if i == 0:
                acc_ref[m] = product
            else:
                acc_ref[m] += product
    part = jnp.concatenate([acc_ref[m].T for m in range(MATS)], axis=0).astype(BF16)
    for r in range(DP):
        out_ref[r] = part


def split_row(row):
    high = row.astype(BF16).astype(F32)
    middle = (row - high).astype(BF16).astype(F32)
    low = row - high - middle
    return jnp.concatenate([high, middle, low, jnp.zeros_like(row)], axis=0)


def half_product(left, corrected_ref, core, turned_ref):
    def columns_step(i, carry):
        products = []
        for g in range(2):
            columns = columns_at(HALF * core + QUARTER * g + TILE * i, TILE)
            for m in range(MATS):
                products.append(
                    lax.dot_general(left[m], corrected_ref[m, :, columns], NN, preferred_element_type=F32)
                )
        turned_ref[columns_at(TILE * i, TILE), :] = jnp.concatenate(products, axis=0).T
        return carry

    lax.fori_loop(0, QUARTER // TILE, columns_step, 0, unroll=True)


def chunked(turned_ref, tail_ref, terms):
    for c in range(CHIPS):
        tail_ref[c, 0:4, :] = turned_ref[HEAD + 4 * c : HEAD + 4 * c + 4, :]
    tail_ref[:, 4:8, :] = jnp.broadcast_to(terms[None], (CHIPS, 4, LANES))
    for n in range(CHIPS // 16):
        head = turned_ref[256 * n : 256 * n + 256, :].reshape(16, 16, LANES)
        yield 16 * n, jnp.concatenate([head, tail_ref[16 * n : 16 * n + 16]], axis=1)


def other_half_kernel(
    parts_ref, corrected_ref, out_ref, summed_ref, row_ref, turned_ref, tail_ref, gram_ref
):
    summed = parts_ref[0].astype(F32)
    for r in range(1, DP):
        summed = summed + parts_ref[r].astype(F32)
    summed_ref[...] = summed
    left = [summed[m * RANK : (m + 1) * RANK] for m in range(MATS)]
    core = lax.axis_index("tensor") % 2
    half_product([x.astype(BF16) for x in left], corrected_ref, 1 - core, turned_ref)

    gram = jnp.concatenate(
        [lax.dot_general(x, x, NT, precision=HIGHEST, preferred_element_type=F32) for x in left], axis=0
    )
    gram_ref[...] = jnp.concatenate([gram[16 * a : 16 * a + 16] for a in range(4)], axis=1)
    row = gram_ref[pl.ds(lax.axis_index("dp"), 1), :]
    row_ref[...] = jnp.broadcast_to(row, row_ref.shape)
    for start, chunks in chunked(turned_ref, tail_ref, split_row(row)):
        out_ref[start : start + 16] = chunks.astype(BF16)


def own_half_kernel(summed_ref, corrected_ref, out_ref, turned_ref, tail_ref):
    left = [summed_ref[m * RANK : (m + 1) * RANK].astype(BF16) for m in range(MATS)]
    half_product(left, corrected_ref, lax.axis_index("tensor") % 2, turned_ref)
    for start, chunks in chunked(turned_ref, tail_ref, jnp.zeros((4, LANES), F32)):
        out_ref[start : start + 16] = chunks


def pair_sum_kernel(own_ref, other_ref, row_ref, out_ref):
    other = other_ref[0].astype(F32)
    row = row_ref[0:1] + (other[20:21] + other[21:22] + other[22:23])
    terms = jnp.concatenate([jnp.zeros((20, LANES), F32), split_row(row)], axis=0)
    is_right = lax.broadcasted_iota(jnp.int32, (1, CHUNK, LANES), 1) < 20
    for start in range(0, CHIPS, 8):
        both = own_ref[start : start + 8] + other_ref[start : start + 8].astype(F32)
        out_ref[start : start + 8] = jnp.where(is_right, both, terms[None]).astype(BF16)


def inverse_factors(grams):
    row = lax.broadcasted_iota(jnp.int32, (RANK, LANES), 0)
    lane = lax.broadcasted_iota(jnp.int32, (RANK, LANES), 1)
    first = (lane // RANK) % 2 == 0
    eye = (lane % RANK == row).astype(F32)
    square = jnp.concatenate(list(grams) + [jnp.zeros((RANK, LANES - BOTH), F32)], axis=1)
    diagonal = square * eye
    trace = [
        jnp.sum(jnp.where(lane // RANK == m, diagonal, 0.0), axis=(0, 1), keepdims=True) for m in range(MATS)
    ]
    shift = 1e-05 * jnp.where(first, trace[0], trace[1]) / RANK
    work = square + jnp.where(lane < BOTH, shift * eye, eye)
    for j in range(RANK - 1):
        column = jnp.where(first, work[:, j : j + 1], work[:, RANK + j : RANK + j + 1])
        pivot_row = work[j : j + 1, :]
        scaled = pivot_row / column[j : j + 1, :]
        work = work - jnp.where(row > j, column, 0.0) * scaled
    pivots = work * eye
    pivot = [
        jnp.sum(jnp.where(lane // RANK == m, pivots, 0.0), axis=1, keepdims=True) for m in range(MATS)
    ]
    return work / jnp.sqrt(jnp.where(first, pivot[0], pivot[1]))


def factor_kernel(parts_ref, summed_ref, out_ref, p_ref, left_ref, gram_ref):
    total = jnp.zeros((CHUNK, LANES), F32)
    for r in range(DP):
        block = parts_ref[CHIPS_X * r].astype(F32)
        for x in range(1, CHIPS_X):
            block = block + parts_ref[CHIPS_X * r + x].astype(F32)
        total = total + block
        gram_ref[r : r + 1, :] = block[20:21] + block[21:22] + block[22:23]
    gram = gram_ref[...]
    gram = jnp.concatenate([gram[:, RANK * a : RANK * a + RANK] for a in range(4)], axis=0)
    inverse = inverse_factors([gram[m * RANK : (m + 1) * RANK] for m in range(MATS)])

    lane = lax.broadcasted_iota(jnp.int32, (RANK, LANES), 1)
    turned = pltpu.roll(inverse, BOTH, 1)
    weights = jnp.concatenate(
        [
            jnp.where(lane // RANK == 2 * g + m, inverse if g else turned, 0.0)
            for g in range(2)
            for m in range(MATS)
        ],
        axis=0,
    )
    right = lax.dot_general(total, weights, NT, precision=HIGHEST, preferred_element_type=F32) / DP
    row = lax.broadcasted_iota(jnp.int32, (CHUNK, LANES), 0)
    right = jnp.where(row < 20, right, 0.0).astype(BF16)
    out_ref[...] = jnp.broadcast_to(right[None], out_ref.shape)
    p = lax.dot_general(
        weights[:BOTH, :BOTH], summed_ref[...], NN, precision=HIGHEST, preferred_element_type=F32
    )
    p_ref[...] = p
    p = p.T
    p = jnp.concatenate([p, p], axis=1)
    lane = lax.broadcasted_iota(jnp.int32, (ROWS, LANES), 1)
    for g in range(2):
        for m in range(MATS):
            left_ref[g, ROWS * m : ROWS * m + ROWS, :] = jnp.where(lane // RANK == 2 * g + m, p, 0.0).astype(BF16)


def half_error(right_ref, left_ref, corrected_ref, out_ref, core, wide_ref, turned_ref, stage_ref, sems):
    for n in range(CHIPS // 16):
        block = right_ref[16 * n : 16 * n + 16].astype(F32)
        wide_ref[256 * n : 256 * n + 256, :] = block[:, 0:16].reshape(256, LANES)
        for c in range(16):
            start = HEAD + 4 * (16 * n + c)
            wide_ref[start : start + 4, :] = block[c, 16:20]
    turned_ref[...] = wide_ref[:QUARTER, :].astype(BF16)

    copies = []
    for i in range(QUARTER // TILE):
        for g in range(2):
            columns = columns_at(HALF * core + QUARTER * g + TILE * i, TILE)
            local_columns = pl.ds(QUARTER * g + TILE * i, TILE)
            rebuilt = lax.dot_general(
                left_ref[g], turned_ref[TILE * i : TILE * i + TILE, :], NT, preferred_element_type=F32
            )
            for m in range(MATS):
                stage_ref[m, :, local_columns] = (
                    corrected_ref[m, :, columns].astype(F32) - rebuilt[ROWS * m : ROWS * m + ROWS]
                ).astype(BF16)
            copy = pltpu.make_async_copy(
                stage_ref.at[:, :, local_columns], out_ref.at[:, :, columns], sems.at[i, g]
            )
            copy.start()
            copies.append(copy)

    me = lax.axis_index("dp") * TENSOR + lax.axis_index("tensor")
    wide_ref[QUARTER:, :] = jnp.zeros((LANES, LANES), F32)
    start = pl.multiple_of(SHARE * (me % (DEVICES // 4)), 8)
    own = wide_ref[pl.ds(start, LANES), :].T
    upper = (me // (DEVICES // 4)) % 2 == 1
    own = jnp.where(upper, own[BOTH:, :SHARE], own[:BOTH, :SHARE])
    for copy in copies:
        copy.wait()
    return own, me // CHIPS == core


def own_error_kernel(right_ref, left_ref, corrected_ref, out_ref, q_ref, *scratch):
    core = lax.axis_index("tensor") % 2
    own, _ = half_error(right_ref, left_ref, corrected_ref, out_ref, core, *scratch)
    q_ref[...] = own


def other_error_kernel(right_ref, left_ref, corrected_ref, q_own_ref, error_ref, out_ref, q_ref, *scratch):
    del error_ref
    core = 1 - lax.axis_index("tensor") % 2
    own, here = half_error(right_ref, left_ref, corrected_ref, out_ref, core, *scratch)
    q_ref[...] = jnp.where(here, own, q_own_ref[...])


WHOLE = pl.BlockSpec(memory_space=pltpu.VMEM)
IN_HBM = pl.BlockSpec(memory_space=pltpu.HBM)


def call(kernel, name, in_specs, out_shape, out_specs=None, scratch=(), flops=0, **extra):
    return pl.pallas_call(
        kernel,
        in_specs=in_specs,
        out_specs=out_specs or [WHOLE] * len(out_shape),
        out_shape=out_shape,
        scratch_shapes=list(scratch),
        compiler_params=pltpu.CompilerParams(vmem_limit_bytes=VMEM_BYTES),
        cost_estimate=pl.CostEstimate(flops=flops, bytes_accessed=4 << 20, transcendentals=0),
        name=name,
        **extra,
    )


def in_hbm(x):
    return pltpu.with_memory_space_constraint(x, pltpu.HBM)


def local(grad, error, q_init):
    steps = WIDTH // STEP
    corrected, part = call(
        left_kernel,
        "left_product",
        [IN_HBM] * 3,
        [pltpu.VMEM((MATS, ROWS, WIDTH), BF16), pltpu.VMEM((DP, BOTH, ROWS), BF16)],
        scratch=[
            pltpu.VMEM((MATS, ROWS, WIDTH), BF16),
            pltpu.VMEM((MATS, RANK, WIDTH), BF16),
            pltpu.VMEM((MATS, ROWS, RANK), F32),
            pltpu.SemaphoreType.DMA((3, steps)),
        ],
    )(in_hbm(grad[0]), in_hbm(error[0]), in_hbm(q_init.transpose(1, 2, 0)))

    parts = lax.all_to_all(part, "dp", 0, 0, tiled=True)

    turned = pltpu.VMEM((QUARTER, LANES), F32)
    tail = pltpu.VMEM((CHIPS, 8, LANES), F32)
    chunks = pltpu.VMEM((CHIPS, CHUNK, LANES), BF16)
    half_flops = 2 * MATS * ROWS * HALF * RANK
    for_other, summed, gram_row = call(
        other_half_kernel,
        "right_product_other",
        [WHOLE] * 2,
        [chunks, pltpu.VMEM((BOTH, ROWS), F32), pltpu.VMEM((8, LANES), F32)],
        scratch=[turned, tail, pltpu.VMEM((16, LANES), F32)],
        flops=half_flops,
    )(parts, corrected)
    from_other = lax.ppermute(for_other, "tensor", CORE_PAIRS)
    own = call(
        own_half_kernel,
        "right_product_own",
        [WHOLE] * 2,
        [pltpu.VMEM((CHIPS, CHUNK, LANES), F32)],
        scratch=[turned, tail],
        flops=half_flops,
    )(summed, corrected)[0]
    partial_q = call(pair_sum_kernel, "pair_sum", [WHOLE] * 3, [chunks])(own, from_other, gram_row)[0]

    partial_q = lax.all_to_all(partial_q, BOTH_AXES, 0, 0, axis_index_groups=SAME_CORE, tiled=True)

    q_own, p_turned, left = call(
        factor_kernel,
        "factor",
        [WHOLE] * 2,
        [chunks, jax.ShapeDtypeStruct((BOTH, ROWS), F32), pltpu.VMEM((2, MATS * ROWS, LANES), BF16)],
        scratch=[pltpu.VMEM((16, LANES), F32)],
    )(partial_q, summed)

    q_half = lax.all_to_all(q_own, BOTH_AXES, 0, 0, axis_index_groups=SAME_CORE, tiled=True)

    q_other = lax.ppermute(q_half, "tensor", CORE_PAIRS)
    scratch = [
        pltpu.VMEM((QUARTER + LANES, LANES), F32),
        pltpu.VMEM((QUARTER, LANES), BF16),
        pltpu.VMEM((MATS, ROWS, HALF), BF16),
        pltpu.SemaphoreType.DMA((QUARTER // TILE, 2)),
    ]
    error_shape = jax.ShapeDtypeStruct((MATS, ROWS, WIDTH), BF16)
    new_error, q_factor = call(
        own_error_kernel,
        "new_error_own",
        [WHOLE] * 3,
        [error_shape, pltpu.VMEM((BOTH, SHARE), F32)],
        [IN_HBM, WHOLE],
        scratch=scratch,
        flops=half_flops,
    )(q_half, left, corrected)
    new_error, q_factor = call(
        other_error_kernel,
        "new_error_other",
        [WHOLE] * 4 + [IN_HBM],
        [error_shape, jax.ShapeDtypeStruct((BOTH, SHARE), F32)],
        [IN_HBM, WHOLE],
        scratch=scratch,
        flops=half_flops,
        input_output_aliases={4: 0},
    )(q_other, left, corrected, q_factor, new_error)

    return (
        new_error[None],
        p_turned.reshape(MATS, RANK, ROWS).transpose(0, 2, 1),
        q_factor.reshape(MATS, RANK, SHARE).transpose(2, 0, 1),
    )


def solution(mesh):
    in_specs = (P("dp", None, "tensor", None), P("dp", None, "tensor", None), P())
    out_specs = (
        P("dp", None, "tensor", None),
        P(None, "tensor", None),
        P(("dp", "tensor"), None, None),
    )
    return jax.shard_map(local, mesh=mesh, in_specs=in_specs, out_specs=out_specs, check_vma=False)
```

```python
import jax
import jax.numpy as jnp
from jax import lax
from jax.experimental import pallas as pl
from jax.experimental.pallas import tpu as pltpu
from jax.sharding import PartitionSpec as P

F32 = jnp.float32
BF16 = jnp.bfloat16
HIGHEST = lax.Precision.HIGHEST
NN = (((1,), (0,)), ((), ()))
NT = (((1,), (1,)), ((), ()))
VMEM_BYTES = 36 * 1024 * 1024

MATS, ROWS, WIDTH, RANK = 2, 384, 5120, 32
BOTH = MATS * RANK
HALF, QUARTER = WIDTH // 2, WIDTH // 4
LANES = 2 * BOTH
DP, TENSOR = 16, 8
DEVICES = DP * TENSOR
CHIPS = DEVICES // 2
CHIPS_X = TENSOR // 2
SHARE = WIDTH // DEVICES
HEAD = 16 * CHIPS
CHUNK = 24
STEP = 512
TILE = 256
BLOCK = 16
PIECES = [(0, 0, 640), (0, 640, 640), (1, 0, 640), (1, 640, 640)]
DP_ORDER = [10, 15, 14, 13, 12, 11, 9, 8, 7, 6, 5, 4, 3, 2, 1, 0]
X_ORDER = [2, 3, 1, 0]
BOTH_AXES = ("dp", "tensor")
CORE_PAIRS = [(i, i ^ 1) for i in range(TENSOR)]
SAME_CORE = [[TENSOR * r + 2 * x + core for r in DP_ORDER for x in X_ORDER] for core in range(2)]


def columns_at(start, size):
    return pl.ds(pl.multiple_of(start, TILE), size)


def left_kernel(grad_ref, error_ref, q_ref, corrected_ref, out_ref, error_vmem, q_vmem, acc_ref, sems):
    starts = range(0, WIDTH, STEP)
    copies = []
    for i, start in enumerate(starts):
        columns = pl.ds(start, STEP)
        pairs = [(q_ref, q_vmem), (grad_ref, corrected_ref), (error_ref, error_vmem)]
        copies.append(
            [
                pltpu.make_async_copy(source.at[:, :, columns], target.at[:, :, columns], sems.at[n, i])
                for n, (source, target) in enumerate(pairs)
            ]
        )
        for copy in copies[-1]:
            copy.start()
    for i, start in enumerate(starts):
        columns = pl.ds(start, STEP)
        for copy in copies[i]:
            copy.wait()
        for m in range(MATS):
            corrected = (corrected_ref[m, :, columns].astype(F32) + error_vmem[m, :, columns].astype(F32)).astype(BF16)
            corrected_ref[m, :, columns] = corrected
            product = lax.dot_general(corrected, q_vmem[m, :, columns], NT, preferred_element_type=F32)
            if i == 0:
                acc_ref[m] = product
            else:
                acc_ref[m] += product
    part = jnp.concatenate([acc_ref[m].T for m in range(MATS)], axis=0).astype(BF16)
    for r in range(DP):
        out_ref[r] = part


def split_row(row):
    high = row.astype(BF16).astype(F32)
    middle = (row - high).astype(BF16).astype(F32)
    low = row - high - middle
    return jnp.concatenate([high, middle, low, jnp.zeros_like(row)], axis=0)


def half_product(left, corrected_ref, core, turned_ref):
    def columns_step(i, carry):
        products = []
        for g in range(2):
            columns = columns_at(HALF * core + QUARTER * g + TILE * i, TILE)
            for m in range(MATS):
                products.append(
                    lax.dot_general(left[m], corrected_ref[m, :, columns], NN, preferred_element_type=F32)
                )
        turned_ref[columns_at(TILE * i, TILE), :] = jnp.concatenate(products, axis=0).T
        return carry

    lax.fori_loop(0, QUARTER // TILE, columns_step, 0, unroll=True)


def chunked(turned_ref, tail_ref, terms):
    for c in range(CHIPS):
        tail_ref[c, 0:4, :] = turned_ref[HEAD + 4 * c : HEAD + 4 * c + 4, :]
    tail_ref[:, 4:8, :] = jnp.broadcast_to(terms[None], (CHIPS, 4, LANES))
    for n in range(CHIPS // 16):
        head = turned_ref[256 * n : 256 * n + 256, :].reshape(16, 16, LANES)
        yield 16 * n, jnp.concatenate([head, tail_ref[16 * n : 16 * n + 16]], axis=1)


def other_half_kernel(
    parts_ref, corrected_ref, out_ref, summed_ref, row_ref, turned_ref, tail_ref, gram_ref
):
    summed = parts_ref[0].astype(F32)
    for r in range(1, DP):
        summed = summed + parts_ref[r].astype(F32)
    summed_ref[...] = summed
    left = [summed[m * RANK : (m + 1) * RANK] for m in range(MATS)]
    core = lax.axis_index("tensor") % 2
    half_product([x.astype(BF16) for x in left], corrected_ref, 1 - core, turned_ref)

    gram = jnp.concatenate(
        [lax.dot_general(x, x, NT, precision=HIGHEST, preferred_element_type=F32) for x in left], axis=0
    )
    gram_ref[...] = jnp.concatenate([gram[16 * a : 16 * a + 16] for a in range(4)], axis=1)
    row = gram_ref[pl.ds(lax.axis_index("dp"), 1), :]
    row_ref[...] = jnp.broadcast_to(row, row_ref.shape)
    for start, chunks in chunked(turned_ref, tail_ref, split_row(row)):
        out_ref[start : start + 16] = chunks.astype(BF16)


def own_half_kernel(summed_ref, corrected_ref, out_ref, turned_ref, tail_ref):
    left = [summed_ref[m * RANK : (m + 1) * RANK].astype(BF16) for m in range(MATS)]
    half_product(left, corrected_ref, lax.axis_index("tensor") % 2, turned_ref)
    for start, chunks in chunked(turned_ref, tail_ref, jnp.zeros((4, LANES), F32)):
        out_ref[start : start + 16] = chunks


def pair_sum_kernel(own_ref, other_ref, row_ref, out_ref):
    other = other_ref[0].astype(F32)
    row = row_ref[0:1] + (other[20:21] + other[21:22] + other[22:23])
    terms = jnp.concatenate([jnp.zeros((20, LANES), F32), split_row(row)], axis=0)
    is_right = lax.broadcasted_iota(jnp.int32, (1, CHUNK, LANES), 1) < 20
    for start in range(0, CHIPS, 8):
        both = own_ref[start : start + 8] + other_ref[start : start + 8].astype(F32)
        out_ref[start : start + 8] = jnp.where(is_right, both, terms[None]).astype(BF16)


def inverse_factors(grams):
    row = lax.broadcasted_iota(jnp.int32, (RANK, LANES), 0)
    lane = lax.broadcasted_iota(jnp.int32, (RANK, LANES), 1)
    first = (lane // RANK) % 2 == 0
    eye = (lane % RANK == row).astype(F32)
    square = jnp.concatenate(list(grams) + [jnp.zeros((RANK, LANES - BOTH), F32)], axis=1)
    diagonal = square * eye
    trace = [
        jnp.sum(jnp.where(lane // RANK == m, diagonal, 0.0), axis=(0, 1), keepdims=True) for m in range(MATS)
    ]
    shift = 1e-05 * jnp.where(first, trace[0], trace[1]) / RANK
    work = square + jnp.where(lane < BOTH, shift * eye, eye)
    for start in range(0, RANK, BLOCK):
        columns = [jnp.where(first, work[:, j : j + 1], work[:, RANK + j : RANK + j + 1]) for j in range(start, start + BLOCK)]
        rows = [work[j : j + 1, :] for j in range(start, start + BLOCK)]
        update = jnp.zeros_like(work)
        for a in range(BLOCK):
            inverse_pivot = 1.0 / columns[a][start + a : start + a + 1, :]
            scaled = rows[a] * inverse_pivot
            below = jnp.where(row > start + a, columns[a], 0.0)
            update = update + below * scaled
            for b in range(a + 1, BLOCK):
                value = columns[a][start + b : start + b + 1, :]
                rows[b] = rows[b] - value * scaled
                columns[b] = columns[b] - below * (value * inverse_pivot)
        work = work - update
    pivots = work * eye
    pivot = [
        jnp.sum(jnp.where(lane // RANK == m, pivots, 0.0), axis=1, keepdims=True) for m in range(MATS)
    ]
    return work / jnp.sqrt(jnp.where(first, pivot[0], pivot[1]))


def factor_kernel(parts_ref, summed_ref, out_ref, p_ref, left_ref, gram_ref):
    total = jnp.zeros((CHUNK, LANES), F32)
    for i, r in enumerate(DP_ORDER):
        block = parts_ref[CHIPS_X * i].astype(F32)
        for x in range(1, CHIPS_X):
            block = block + parts_ref[CHIPS_X * i + x].astype(F32)
        total = total + block
        gram_ref[r : r + 1, :] = block[20:21] + block[21:22] + block[22:23]
    gram = gram_ref[...]
    gram = jnp.concatenate([gram[:, RANK * a : RANK * a + RANK] for a in range(4)], axis=0)
    inverse = inverse_factors([gram[m * RANK : (m + 1) * RANK] for m in range(MATS)])

    lane = lax.broadcasted_iota(jnp.int32, (RANK, LANES), 1)
    turned = pltpu.roll(inverse, BOTH, 1)
    weights = jnp.concatenate(
        [
            jnp.where(lane // RANK == 2 * g + m, inverse if g else turned, 0.0)
            for g in range(2)
            for m in range(MATS)
        ],
        axis=0,
    )
    right = lax.dot_general(total, weights, NT, precision=HIGHEST, preferred_element_type=F32) / DP
    row = lax.broadcasted_iota(jnp.int32, (CHUNK, LANES), 0)
    right = jnp.where(row < 20, right, 0.0).astype(BF16)
    out_ref[...] = jnp.broadcast_to(right[None], out_ref.shape)
    p = lax.dot_general(
        weights[:BOTH, :BOTH], summed_ref[...], NN, precision=HIGHEST, preferred_element_type=F32
    )
    p_ref[...] = p
    p = p.T
    p = jnp.concatenate([p, p], axis=1)
    lane = lax.broadcasted_iota(jnp.int32, (ROWS, LANES), 1)
    for g in range(2):
        for m in range(MATS):
            left_ref[g, ROWS * m : ROWS * m + ROWS, :] = jnp.where(lane // RANK == 2 * g + m, p, 0.0).astype(BF16)


def half_error(right_ref, left_ref, corrected_ref, out_ref, core, wide_ref, turned_ref, stage_ref, sems):
    for n in range(CHIPS // 16):
        block = right_ref[16 * n : 16 * n + 16].astype(F32)
        wide_ref[256 * n : 256 * n + 256, :] = block[:, 0:16].reshape(256, LANES)
        for c in range(16):
            start = HEAD + 4 * (16 * n + c)
            wide_ref[start : start + 4, :] = block[c, 16:20]
    turned_ref[...] = wide_ref[:QUARTER, :].astype(BF16)

    copies = []
    for n, (g, first, size) in enumerate(PIECES):
        columns = pl.ds(pl.multiple_of(HALF * core + QUARTER * g + first, LANES), size)
        local_columns = pl.ds(QUARTER * g + first, size)
        rebuilt = lax.dot_general(
            left_ref[g], turned_ref[first : first + size, :], NT, preferred_element_type=F32
        )
        for m in range(MATS):
            stage_ref[m, :, local_columns] = (
                corrected_ref[m, :, columns].astype(F32) - rebuilt[ROWS * m : ROWS * m + ROWS]
            ).astype(BF16)
        copy = pltpu.make_async_copy(stage_ref.at[:, :, local_columns], out_ref.at[:, :, columns], sems.at[n])
        copy.start()
        copies.append(copy)

    me = lax.axis_index("dp") * TENSOR + lax.axis_index("tensor")
    wide_ref[QUARTER:, :] = jnp.zeros((LANES, LANES), F32)
    start = pl.multiple_of(SHARE * (me % (DEVICES // 4)), 8)
    own = wide_ref[pl.ds(start, LANES), :].T
    upper = (me // (DEVICES // 4)) % 2 == 1
    own = jnp.where(upper, own[BOTH:, :SHARE], own[:BOTH, :SHARE])
    for copy in copies:
        copy.wait()
    return own, me // CHIPS == core


def own_error_kernel(right_ref, left_ref, corrected_ref, out_ref, q_ref, *scratch):
    core = lax.axis_index("tensor") % 2
    own, _ = half_error(right_ref, left_ref, corrected_ref, out_ref, core, *scratch)
    q_ref[...] = own


def other_error_kernel(right_ref, left_ref, corrected_ref, q_own_ref, error_ref, out_ref, q_ref, *scratch):
    del error_ref
    core = 1 - lax.axis_index("tensor") % 2
    own, here = half_error(right_ref, left_ref, corrected_ref, out_ref, core, *scratch)
    q_ref[...] = jnp.where(here, own, q_own_ref[...])


WHOLE = pl.BlockSpec(memory_space=pltpu.VMEM)
IN_HBM = pl.BlockSpec(memory_space=pltpu.HBM)


def call(kernel, name, in_specs, out_shape, out_specs=None, scratch=(), flops=0, **extra):
    return pl.pallas_call(
        kernel,
        in_specs=in_specs,
        out_specs=out_specs or [WHOLE] * len(out_shape),
        out_shape=out_shape,
        scratch_shapes=list(scratch),
        compiler_params=pltpu.CompilerParams(vmem_limit_bytes=VMEM_BYTES),
        cost_estimate=pl.CostEstimate(flops=flops, bytes_accessed=4 << 20, transcendentals=0),
        name=name,
        **extra,
    )


def in_hbm(x):
    return pltpu.with_memory_space_constraint(x, pltpu.HBM)


def local(grad, error, q_init):
    steps = WIDTH // STEP
    corrected, part = call(
        left_kernel,
        "left_product",
        [IN_HBM] * 3,
        [pltpu.VMEM((MATS, ROWS, WIDTH), BF16), pltpu.VMEM((DP, BOTH, ROWS), BF16)],
        scratch=[
            pltpu.VMEM((MATS, ROWS, WIDTH), BF16),
            pltpu.VMEM((MATS, RANK, WIDTH), BF16),
            pltpu.VMEM((MATS, ROWS, RANK), F32),
            pltpu.SemaphoreType.DMA((3, steps)),
        ],
    )(in_hbm(grad[0]), in_hbm(error[0]), in_hbm(q_init.transpose(1, 2, 0)))

    parts = lax.all_to_all(part, "dp", 0, 0, axis_index_groups=[DP_ORDER], tiled=True)

    turned = pltpu.VMEM((QUARTER, LANES), F32)
    tail = pltpu.VMEM((CHIPS, 8, LANES), F32)
    chunks = pltpu.VMEM((CHIPS, CHUNK, LANES), BF16)
    half_flops = 2 * MATS * ROWS * HALF * RANK
    for_other, summed, gram_row = call(
        other_half_kernel,
        "right_product_other",
        [WHOLE] * 2,
        [chunks, pltpu.VMEM((BOTH, ROWS), F32), pltpu.VMEM((8, LANES), F32)],
        scratch=[turned, tail, pltpu.VMEM((16, LANES), F32)],
        flops=half_flops,
    )(parts, corrected)
    from_other = lax.ppermute(for_other, "tensor", CORE_PAIRS)
    own = call(
        own_half_kernel,
        "right_product_own",
        [WHOLE] * 2,
        [pltpu.VMEM((CHIPS, CHUNK, LANES), F32)],
        scratch=[turned, tail],
        flops=half_flops,
    )(summed, corrected)[0]
    partial_q = call(pair_sum_kernel, "pair_sum", [WHOLE] * 3, [chunks])(own, from_other, gram_row)[0]

    partial_q = lax.all_to_all(partial_q, BOTH_AXES, 0, 0, axis_index_groups=SAME_CORE, tiled=True)

    q_own, p_turned, left = call(
        factor_kernel,
        "factor",
        [WHOLE] * 2,
        [chunks, jax.ShapeDtypeStruct((BOTH, ROWS), F32), pltpu.VMEM((2, MATS * ROWS, LANES), BF16)],
        scratch=[pltpu.VMEM((16, LANES), F32)],
    )(partial_q, summed)

    q_half = lax.all_to_all(q_own, BOTH_AXES, 0, 0, axis_index_groups=SAME_CORE, tiled=True)

    q_other = lax.ppermute(q_half, "tensor", CORE_PAIRS)
    scratch = [
        pltpu.VMEM((QUARTER + LANES, LANES), F32),
        pltpu.VMEM((QUARTER, LANES), BF16),
        pltpu.VMEM((MATS, ROWS, HALF), BF16),
        pltpu.SemaphoreType.DMA((len(PIECES),)),
    ]
    error_shape = jax.ShapeDtypeStruct((MATS, ROWS, WIDTH), BF16)
    new_error, q_factor = call(
        own_error_kernel,
        "new_error_own",
        [WHOLE] * 3,
        [error_shape, pltpu.VMEM((BOTH, SHARE), F32)],
        [IN_HBM, WHOLE],
        scratch=scratch,
        flops=half_flops,
    )(q_half, left, corrected)
    new_error, q_factor = call(
        other_error_kernel,
        "new_error_other",
        [WHOLE] * 4 + [IN_HBM],
        [error_shape, jax.ShapeDtypeStruct((BOTH, SHARE), F32)],
        [IN_HBM, WHOLE],
        scratch=scratch,
        flops=half_flops,
        input_output_aliases={4: 0},
    )(q_other, left, corrected, q_factor, new_error)

    return (
        new_error[None],
        p_turned.reshape(MATS, RANK, ROWS).transpose(0, 2, 1),
        q_factor.reshape(MATS, RANK, SHARE).transpose(2, 0, 1),
    )


def solution(mesh):
    in_specs = (P("dp", None, "tensor", None), P("dp", None, "tensor", None), P())
    out_specs = (
        P("dp", None, "tensor", None),
        P(None, "tensor", None),
        P(("dp", "tensor"), None, None),
    )
    return jax.shard_map(local, mesh=mesh, in_specs=in_specs, out_specs=out_specs, check_vma=False)
```

```python
import jax
import jax.numpy as jnp
from jax import lax
from jax.experimental import pallas as pl
from jax.experimental.pallas import tpu as pltpu
from jax.sharding import PartitionSpec as P

F32 = jnp.float32
BF16 = jnp.bfloat16
HIGHEST = lax.Precision.HIGHEST
NN = (((1,), (0,)), ((), ()))
NT = (((1,), (1,)), ((), ()))
VMEM_BYTES = 36 * 1024 * 1024

MATS, ROWS, WIDTH, RANK = 2, 384, 5120, 32
BOTH = MATS * RANK
HALF, QUARTER = WIDTH // 2, WIDTH // 4
LANES = 2 * BOTH
DP, TENSOR = 16, 8
DEVICES = DP * TENSOR
CHIPS = DEVICES // 2
CHIPS_X = TENSOR // 2
SHARE = WIDTH // DEVICES
HEAD = 16 * CHIPS
CHUNK = 24
READS = [1024] * 4 + [512, 256, 256]
TILE = 256
BLOCK = 16
PIECES = [(0, 0, 640), (0, 640, 640), (1, 0, 640), (1, 640, 640)]
DP_ORDER = [10, 15, 14, 13, 12, 11, 9, 8, 7, 6, 5, 4, 3, 2, 1, 0]
CHIP_ORDER = [
    42, 52, 40, 44, 60, 63, 24, 54, 0, 11, 45, 56, 18, 34, 10, 55,
    46, 38, 15, 31, 57, 61, 36, 5, 17, 62, 21, 22, 49, 6, 1, 29,
    41, 33, 28, 30, 51, 8, 2, 26, 32, 48, 7, 27, 23, 25, 4, 39,
    37, 14, 59, 19, 43, 16, 47, 20, 3, 53, 13, 50, 35, 9, 12, 58,
]
BOTH_AXES = ("dp", "tensor")
CORE_PAIRS = [(i, i ^ 1) for i in range(TENSOR)]
SAME_CORE = [[2 * chip + core for chip in CHIP_ORDER] for core in range(2)]


def columns_at(start, size):
    return pl.ds(pl.multiple_of(start, TILE), size)


def left_kernel(grad_ref, error_ref, q_ref, corrected_ref, out_ref, error_vmem, q_vmem, acc_ref, sems):
    reads = [pl.ds(sum(READS[:i]), size) for i, size in enumerate(READS)]
    copies = []
    for i, columns in enumerate(reads):
        pairs = [(q_ref, q_vmem), (grad_ref, corrected_ref), (error_ref, error_vmem)]
        copies.append(
            [
                pltpu.make_async_copy(source.at[:, :, columns], target.at[:, :, columns], sems.at[n, i])
                for n, (source, target) in enumerate(pairs)
            ]
        )
        for copy in copies[-1]:
            copy.start()
    for i, columns in enumerate(reads):
        for copy in copies[i]:
            copy.wait()
        for m in range(MATS):
            corrected = (corrected_ref[m, :, columns].astype(F32) + error_vmem[m, :, columns].astype(F32)).astype(BF16)
            corrected_ref[m, :, columns] = corrected
            product = lax.dot_general(corrected, q_vmem[m, :, columns], NT, preferred_element_type=F32)
            if i == 0:
                acc_ref[m] = product
            else:
                acc_ref[m] += product
    part = jnp.concatenate([acc_ref[m].T for m in range(MATS)], axis=0).astype(BF16)
    for r in range(DP):
        out_ref[r] = part


def split_row(row):
    high = row.astype(BF16).astype(F32)
    middle = (row - high).astype(BF16).astype(F32)
    low = row - high - middle
    return jnp.concatenate([high, middle, low, jnp.zeros_like(row)], axis=0)


def half_product(left, corrected_ref, core, turned_ref):
    def columns_step(i, carry):
        products = []
        for g in range(2):
            columns = columns_at(HALF * core + QUARTER * g + TILE * i, TILE)
            for m in range(MATS):
                products.append(
                    lax.dot_general(left[m], corrected_ref[m, :, columns], NN, preferred_element_type=F32)
                )
        turned_ref[columns_at(TILE * i, TILE), :] = jnp.concatenate(products, axis=0).T
        return carry

    lax.fori_loop(0, QUARTER // TILE, columns_step, 0, unroll=True)


def chunked(turned_ref, tail_ref, terms):
    for c in range(CHIPS):
        tail_ref[c, 0:4, :] = turned_ref[HEAD + 4 * c : HEAD + 4 * c + 4, :]
    tail_ref[:, 4:8, :] = jnp.broadcast_to(terms[None], (CHIPS, 4, LANES))
    for n in range(CHIPS // 16):
        head = turned_ref[256 * n : 256 * n + 256, :].reshape(16, 16, LANES)
        yield 16 * n, jnp.concatenate([head, tail_ref[16 * n : 16 * n + 16]], axis=1)


def other_half_kernel(
    parts_ref, corrected_ref, out_ref, summed_ref, row_ref, turned_ref, tail_ref, gram_ref
):
    summed = parts_ref[0].astype(F32)
    for r in range(1, DP):
        summed = summed + parts_ref[r].astype(F32)
    summed_ref[...] = summed
    left = [summed[m * RANK : (m + 1) * RANK] for m in range(MATS)]
    core = lax.axis_index("tensor") % 2
    half_product([x.astype(BF16) for x in left], corrected_ref, 1 - core, turned_ref)

    gram = jnp.concatenate(
        [lax.dot_general(x, x, NT, precision=HIGHEST, preferred_element_type=F32) for x in left], axis=0
    )
    gram_ref[...] = jnp.concatenate([gram[16 * a : 16 * a + 16] for a in range(4)], axis=1)
    row = gram_ref[pl.ds(lax.axis_index("dp"), 1), :]
    row_ref[...] = jnp.broadcast_to(row, row_ref.shape)
    for start, chunks in chunked(turned_ref, tail_ref, split_row(row)):
        out_ref[start : start + 16] = chunks.astype(BF16)


def own_half_kernel(summed_ref, corrected_ref, out_ref, turned_ref, tail_ref):
    left = [summed_ref[m * RANK : (m + 1) * RANK].astype(BF16) for m in range(MATS)]
    half_product(left, corrected_ref, lax.axis_index("tensor") % 2, turned_ref)
    for start, chunks in chunked(turned_ref, tail_ref, jnp.zeros((4, LANES), F32)):
        out_ref[start : start + 16] = chunks


def pair_sum_kernel(own_ref, other_ref, row_ref, out_ref):
    other = other_ref[0].astype(F32)
    row = row_ref[0:1] + (other[20:21] + other[21:22] + other[22:23])
    terms = jnp.concatenate([jnp.zeros((20, LANES), F32), split_row(row)], axis=0)
    is_right = lax.broadcasted_iota(jnp.int32, (1, CHUNK, LANES), 1) < 20
    for start in range(0, CHIPS, 8):
        both = own_ref[start : start + 8] + other_ref[start : start + 8].astype(F32)
        out_ref[start : start + 8] = jnp.where(is_right, both, terms[None]).astype(BF16)


def inverse_factors(grams):
    row = lax.broadcasted_iota(jnp.int32, (RANK, LANES), 0)
    lane = lax.broadcasted_iota(jnp.int32, (RANK, LANES), 1)
    first = (lane // RANK) % 2 == 0
    eye = (lane % RANK == row).astype(F32)
    square = jnp.concatenate(list(grams) + [jnp.zeros((RANK, LANES - BOTH), F32)], axis=1)
    diagonal = square * eye
    trace = [
        jnp.sum(jnp.where(lane // RANK == m, diagonal, 0.0), axis=(0, 1), keepdims=True) for m in range(MATS)
    ]
    shift = 1e-05 * jnp.where(first, trace[0], trace[1]) / RANK
    work = square + jnp.where(lane < BOTH, shift * eye, eye)
    for start in range(0, RANK, BLOCK):
        columns = [jnp.where(first, work[:, j : j + 1], work[:, RANK + j : RANK + j + 1]) for j in range(start, start + BLOCK)]
        rows = [work[j : j + 1, :] for j in range(start, start + BLOCK)]
        update = jnp.zeros_like(work)
        for a in range(BLOCK):
            inverse_pivot = 1.0 / columns[a][start + a : start + a + 1, :]
            scaled = rows[a] * inverse_pivot
            below = jnp.where(row > start + a, columns[a], 0.0)
            update = update + below * scaled
            for b in range(a + 1, BLOCK):
                value = columns[a][start + b : start + b + 1, :]
                rows[b] = rows[b] - value * scaled
                columns[b] = columns[b] - below * (value * inverse_pivot)
        work = work - update
    pivots = work * eye
    pivot = [
        jnp.sum(jnp.where(lane // RANK == m, pivots, 0.0), axis=1, keepdims=True) for m in range(MATS)
    ]
    return work / jnp.sqrt(jnp.where(first, pivot[0], pivot[1]))


def factor_kernel(parts_ref, summed_ref, out_ref, p_ref, left_ref, gram_ref):
    total = jnp.zeros((CHUNK, LANES), F32)
    for r in range(DP):
        places = [CHIP_ORDER.index(CHIPS_X * r + x) for x in range(CHIPS_X)]
        block = parts_ref[places[0]].astype(F32)
        for place in places[1:]:
            block = block + parts_ref[place].astype(F32)
        total = total + block
        gram_ref[r : r + 1, :] = block[20:21] + block[21:22] + block[22:23]
    gram = gram_ref[...]
    gram = jnp.concatenate([gram[:, RANK * a : RANK * a + RANK] for a in range(4)], axis=0)
    inverse = inverse_factors([gram[m * RANK : (m + 1) * RANK] for m in range(MATS)])

    lane = lax.broadcasted_iota(jnp.int32, (RANK, LANES), 1)
    turned = pltpu.roll(inverse, BOTH, 1)
    weights = jnp.concatenate(
        [
            jnp.where(lane // RANK == 2 * g + m, inverse if g else turned, 0.0)
            for g in range(2)
            for m in range(MATS)
        ],
        axis=0,
    )
    right = lax.dot_general(total, weights, NT, precision=HIGHEST, preferred_element_type=F32) / DP
    row = lax.broadcasted_iota(jnp.int32, (CHUNK, LANES), 0)
    right = jnp.where(row < 20, right, 0.0).astype(BF16)
    out_ref[...] = jnp.broadcast_to(right[None], out_ref.shape)
    p = lax.dot_general(
        weights[:BOTH, :BOTH], summed_ref[...], NN, precision=HIGHEST, preferred_element_type=F32
    )
    p_ref[...] = p
    p = p.T
    p = jnp.concatenate([p, p], axis=1)
    lane = lax.broadcasted_iota(jnp.int32, (ROWS, LANES), 1)
    for g in range(2):
        for m in range(MATS):
            left_ref[g, ROWS * m : ROWS * m + ROWS, :] = jnp.where(lane // RANK == 2 * g + m, p, 0.0).astype(BF16)


def piece_copy(stage, out_ref, core, piece, sem):
    g, first, size = piece
    columns = pl.ds(pl.multiple_of(HALF * core + QUARTER * g + first, LANES), size)
    return pltpu.make_async_copy(stage, out_ref.at[:, :, columns], sem)


def half_error(right_ref, left_ref, corrected_ref, out_ref, core, wide_ref, turned_ref, stage_ref, sems, rest_ref=None):
    for n in range(CHIPS // 16):
        block = right_ref[16 * n : 16 * n + 16].astype(F32)
        wide_ref[256 * n : 256 * n + 256, :] = block[:, 0:16].reshape(256, LANES)
        for c in range(16):
            start = HEAD + 4 * (16 * n + c)
            wide_ref[start : start + 4, :] = block[c, 16:20]
    turned_ref[...] = wide_ref[:QUARTER, :].astype(BF16)

    copies = []
    for n, (g, first, size) in enumerate(PIECES):
        columns = pl.ds(pl.multiple_of(HALF * core + QUARTER * g + first, LANES), size)
        rebuilt = lax.dot_general(
            left_ref[g], turned_ref[first : first + size, :], NT, preferred_element_type=F32
        )
        keep = rest_ref is not None and n == len(PIECES) - 1
        stage = rest_ref if keep else stage_ref.at[:, :, pl.ds(QUARTER * g + first, size)]
        for m in range(MATS):
            stage[m] = (
                corrected_ref[m, :, columns].astype(F32) - rebuilt[ROWS * m : ROWS * m + ROWS]
            ).astype(BF16)
        if not keep:
            copies.append(piece_copy(stage, out_ref, core, PIECES[n], sems.at[n]))
            copies[-1].start()

    me = lax.axis_index("dp") * TENSOR + lax.axis_index("tensor")
    wide_ref[QUARTER:, :] = jnp.zeros((LANES, LANES), F32)
    start = pl.multiple_of(SHARE * (me % (DEVICES // 4)), 8)
    own = wide_ref[pl.ds(start, LANES), :].T
    upper = (me // (DEVICES // 4)) % 2 == 1
    return copies, jnp.where(upper, own[BOTH:, :SHARE], own[:BOTH, :SHARE])


def own_error_kernel(
    right_ref, left_ref, corrected_ref, p_ref, out_ref, q_ref, rest_ref, p_out_ref, *scratch
):
    *scratch, p_sem = scratch
    p_copy = pltpu.make_async_copy(p_ref, p_out_ref, p_sem)
    p_copy.start()
    core = lax.axis_index("tensor") % 2
    copies, q_ref[...] = half_error(right_ref, left_ref, corrected_ref, out_ref, core, *scratch, rest_ref)
    for copy in [*copies, p_copy]:
        copy.wait()


def other_error_kernel(
    right_ref, left_ref, corrected_ref, q_own_ref, rest_ref, error_ref, out_ref, q_out_ref, *scratch
):
    del error_ref
    *scratch, q_ref, rest_sem, q_sem = scratch
    core = lax.axis_index("tensor") % 2
    rest_copy = piece_copy(rest_ref, out_ref, core, PIECES[-1], rest_sem)
    rest_copy.start()
    copies, other = half_error(right_ref, left_ref, corrected_ref, out_ref, 1 - core, *scratch)
    me = lax.axis_index("dp") * TENSOR + lax.axis_index("tensor")
    q_ref[...] = jnp.where(me // CHIPS == core, q_own_ref[...], other)
    q_copy = pltpu.make_async_copy(q_ref, q_out_ref, q_sem)
    q_copy.start()
    for copy in [rest_copy, *copies, q_copy]:
        copy.wait()


WHOLE = pl.BlockSpec(memory_space=pltpu.VMEM)
IN_HBM = pl.BlockSpec(memory_space=pltpu.HBM)


def call(kernel, name, in_specs, out_shape, out_specs=None, scratch=(), flops=0, **extra):
    return pl.pallas_call(
        kernel,
        in_specs=in_specs,
        out_specs=out_specs or [WHOLE] * len(out_shape),
        out_shape=out_shape,
        scratch_shapes=list(scratch),
        compiler_params=pltpu.CompilerParams(vmem_limit_bytes=VMEM_BYTES),
        cost_estimate=pl.CostEstimate(flops=flops, bytes_accessed=4 << 20, transcendentals=0),
        name=name,
        **extra,
    )


def in_hbm(x):
    return pltpu.with_memory_space_constraint(x, pltpu.HBM)


def local(grad, error, q_init):
    corrected, part = call(
        left_kernel,
        "left_product",
        [IN_HBM] * 3,
        [pltpu.VMEM((MATS, ROWS, WIDTH), BF16), pltpu.VMEM((DP, BOTH, ROWS), BF16)],
        scratch=[
            pltpu.VMEM((MATS, ROWS, WIDTH), BF16),
            pltpu.VMEM((MATS, RANK, WIDTH), BF16),
            pltpu.VMEM((MATS, ROWS, RANK), F32),
            pltpu.SemaphoreType.DMA((3, len(READS))),
        ],
    )(in_hbm(grad[0]), in_hbm(error[0]), in_hbm(q_init.transpose(1, 2, 0)))

    parts = lax.all_to_all(part, "dp", 0, 0, axis_index_groups=[DP_ORDER], tiled=True)

    turned = pltpu.VMEM((QUARTER, LANES), F32)
    tail = pltpu.VMEM((CHIPS, 8, LANES), F32)
    chunks = pltpu.VMEM((CHIPS, CHUNK, LANES), BF16)
    half_flops = 2 * MATS * ROWS * HALF * RANK
    for_other, summed, gram_row = call(
        other_half_kernel,
        "right_product_other",
        [WHOLE] * 2,
        [chunks, pltpu.VMEM((BOTH, ROWS), F32), pltpu.VMEM((8, LANES), F32)],
        scratch=[turned, tail, pltpu.VMEM((16, LANES), F32)],
        flops=half_flops,
    )(parts, corrected)
    from_other = lax.ppermute(for_other, "tensor", CORE_PAIRS)
    own = call(
        own_half_kernel,
        "right_product_own",
        [WHOLE] * 2,
        [pltpu.VMEM((CHIPS, CHUNK, LANES), F32)],
        scratch=[turned, tail],
        flops=half_flops,
    )(summed, corrected)[0]
    partial_q = call(pair_sum_kernel, "pair_sum", [WHOLE] * 3, [chunks])(own, from_other, gram_row)[0]

    partial_q = lax.all_to_all(partial_q, BOTH_AXES, 0, 0, axis_index_groups=SAME_CORE, tiled=True)

    q_own, p_turned, left = call(
        factor_kernel,
        "factor",
        [WHOLE] * 2,
        [chunks, pltpu.VMEM((BOTH, ROWS), F32), pltpu.VMEM((2, MATS * ROWS, LANES), BF16)],
        scratch=[pltpu.VMEM((16, LANES), F32)],
    )(partial_q, summed)

    q_half = lax.all_to_all(q_own, BOTH_AXES, 0, 0, axis_index_groups=SAME_CORE, tiled=True)

    q_other = lax.ppermute(q_half, "tensor", CORE_PAIRS)
    scratch = [
        pltpu.VMEM((QUARTER + LANES, LANES), F32),
        pltpu.VMEM((QUARTER, LANES), BF16),
        pltpu.VMEM((MATS, ROWS, HALF), BF16),
        pltpu.SemaphoreType.DMA((len(PIECES),)),
    ]
    error_shape = jax.ShapeDtypeStruct((MATS, ROWS, WIDTH), BF16)
    factor_shape = jax.ShapeDtypeStruct((BOTH, ROWS), F32)
    rest_shape = pltpu.VMEM((MATS, ROWS, PIECES[-1][2]), BF16)
    new_error, q_factor, rest, p_factor = call(
        own_error_kernel,
        "new_error_own",
        [WHOLE] * 4,
        [error_shape, pltpu.VMEM((BOTH, SHARE), F32), rest_shape, factor_shape],
        [IN_HBM, WHOLE, WHOLE, IN_HBM],
        scratch=[*scratch, pltpu.SemaphoreType.DMA],
        flops=half_flops,
    )(q_half, left, corrected, p_turned)
    new_error, q_factor = call(
        other_error_kernel,
        "new_error_other",
        [WHOLE] * 5 + [IN_HBM],
        [error_shape, jax.ShapeDtypeStruct((BOTH, SHARE), F32)],
        [IN_HBM, IN_HBM],
        scratch=[*scratch, pltpu.VMEM((BOTH, SHARE), F32), pltpu.SemaphoreType.DMA, pltpu.SemaphoreType.DMA],
        flops=half_flops,
        input_output_aliases={5: 0},
    )(q_other, left, corrected, q_factor, rest, new_error)

    return (
        new_error[None],
        p_factor.reshape(MATS, RANK, ROWS).transpose(0, 2, 1),
        q_factor.reshape(MATS, RANK, SHARE).transpose(2, 0, 1),
    )


def solution(mesh):
    in_specs = (P("dp", None, "tensor", None), P("dp", None, "tensor", None), P())
    out_specs = (
        P("dp", None, "tensor", None),
        P(None, "tensor", None),
        P(("dp", "tensor"), None, None),
    )
    return jax.shard_map(local, mesh=mesh, in_specs=in_specs, out_specs=out_specs, check_vma=False)
```

```python
import jax
import jax.numpy as jnp
from jax import lax
from jax.experimental import pallas as pl
from jax.experimental.pallas import tpu as pltpu
from jax.sharding import PartitionSpec as P

F32 = jnp.float32
BF16 = jnp.bfloat16
HIGHEST = lax.Precision.HIGHEST
NN = (((1,), (0,)), ((), ()))
NT = (((1,), (1,)), ((), ()))
VMEM_BYTES = 36 * 1024 * 1024

MATS, ROWS, WIDTH, RANK = 2, 384, 5120, 32
BOTH = MATS * RANK
HALF, QUARTER = WIDTH // 2, WIDTH // 4
LANES = 2 * BOTH
DP, TENSOR = 16, 8
DEVICES = DP * TENSOR
CHIPS = DEVICES // 2
CHIPS_X = TENSOR // 2
SHARE = WIDTH // DEVICES
HEAD = 16 * CHIPS
CHUNK = 24
READS = [1280, 1280, 1280, 768, 512]
TILE = 256
BLOCK = 16
PIECES = [(0, 0, 640), (0, 640, 640), (1, 0, 640), (1, 640, 640)]
DP_ORDER = [10, 0, 14, 13, 7, 1, 2, 3, 15, 9, 12, 6, 8, 11, 5, 4]
CHIP_ORDER = [
    42, 52, 40, 44, 60, 63, 24, 54, 0, 11, 45, 56, 18, 34, 10, 55,
    46, 38, 15, 31, 57, 61, 36, 5, 17, 62, 21, 22, 49, 6, 1, 29,
    41, 33, 28, 30, 51, 8, 2, 26, 32, 48, 7, 27, 23, 25, 4, 39,
    37, 14, 59, 19, 43, 16, 47, 20, 3, 53, 13, 50, 35, 9, 12, 58,
]
BOTH_AXES = ("dp", "tensor")
CORE_PAIRS = [(i, i ^ 1) for i in range(TENSOR)]
SAME_CORE = [[2 * chip + core for chip in CHIP_ORDER] for core in range(2)]


def columns_at(start, size):
    return pl.ds(pl.multiple_of(start, TILE), size)


def left_kernel(grad_ref, error_ref, q_ref, corrected_ref, out_ref, error_vmem, q_vmem, acc_ref, sems):
    reads = [pl.ds(sum(READS[:i]), size) for i, size in enumerate(READS)]
    copies = []
    for i, columns in enumerate(reads):
        pairs = [(q_ref, q_vmem), (grad_ref, corrected_ref), (error_ref, error_vmem)]
        copies.append(
            [
                pltpu.make_async_copy(source.at[:, :, columns], target.at[:, :, columns], sems.at[n, i])
                for n, (source, target) in enumerate(pairs)
            ]
        )
        for copy in copies[-1]:
            copy.start()
    for i, columns in enumerate(reads):
        for copy in copies[i]:
            copy.wait()
        for m in range(MATS):
            corrected = (corrected_ref[m, :, columns].astype(F32) + error_vmem[m, :, columns].astype(F32)).astype(BF16)
            corrected_ref[m, :, columns] = corrected
            product = lax.dot_general(corrected, q_vmem[m, :, columns], NT, preferred_element_type=F32)
            if i == 0:
                acc_ref[m] = product
            else:
                acc_ref[m] += product
    part = jnp.concatenate([acc_ref[m].T for m in range(MATS)], axis=0).astype(BF16)
    for r in range(DP):
        out_ref[r] = part


def split_row(row):
    high = row.astype(BF16).astype(F32)
    middle = (row - high).astype(BF16).astype(F32)
    low = row - high - middle
    return jnp.concatenate([high, middle, low, jnp.zeros_like(row)], axis=0)


def half_product(left, corrected_ref, core, turned_ref):
    def columns_step(i, carry):
        products = []
        for g in range(2):
            columns = columns_at(HALF * core + QUARTER * g + TILE * i, TILE)
            for m in range(MATS):
                products.append(
                    lax.dot_general(left[m], corrected_ref[m, :, columns], NN, preferred_element_type=F32)
                )
        turned_ref[columns_at(TILE * i, TILE), :] = jnp.concatenate(products, axis=0).T
        return carry

    lax.fori_loop(0, QUARTER // TILE, columns_step, 0, unroll=True)


def chunked(turned_ref, tail_ref, terms):
    for n in range(4):
        tail_ref[pl.ds(n, CHIPS, stride=8), :] = turned_ref[HEAD + CHIPS * n : HEAD + CHIPS * n + CHIPS, :]
        tail_ref[pl.ds(n + 4, CHIPS, stride=8), :] = jnp.broadcast_to(terms[n : n + 1], (CHIPS, LANES))
    for n in range(CHIPS // 16):
        head = turned_ref[256 * n : 256 * n + 256, :].reshape(16, 16, LANES)
        tail = tail_ref[128 * n : 128 * n + 128, :].reshape(16, 8, LANES)
        yield 16 * n, jnp.concatenate([head, tail], axis=1)


def other_half_kernel(
    parts_ref, corrected_ref, out_ref, summed_ref, row_ref, turned_ref, tail_ref, gram_ref
):
    summed = parts_ref[0].astype(F32)
    for r in range(1, DP):
        summed = summed + parts_ref[r].astype(F32)
    summed_ref[...] = summed
    left = [summed[m * RANK : (m + 1) * RANK] for m in range(MATS)]
    core = lax.axis_index("tensor") % 2
    half_product([x.astype(BF16) for x in left], corrected_ref, 1 - core, turned_ref)

    gram = jnp.concatenate(
        [lax.dot_general(x, x, NT, precision=HIGHEST, preferred_element_type=F32) for x in left], axis=0
    )
    gram_ref[...] = jnp.concatenate([gram[16 * a : 16 * a + 16] for a in range(4)], axis=1)
    row = gram_ref[pl.ds(lax.axis_index("dp"), 1), :]
    row_ref[...] = jnp.broadcast_to(row, row_ref.shape)
    for start, chunks in chunked(turned_ref, tail_ref, split_row(row)):
        out_ref[start : start + 16] = chunks.astype(BF16)


def own_half_kernel(summed_ref, corrected_ref, out_ref, turned_ref, tail_ref):
    left = [summed_ref[m * RANK : (m + 1) * RANK].astype(BF16) for m in range(MATS)]
    half_product(left, corrected_ref, lax.axis_index("tensor") % 2, turned_ref)
    for start, chunks in chunked(turned_ref, tail_ref, jnp.zeros((4, LANES), F32)):
        out_ref[start : start + 16] = chunks


def pair_sum_kernel(own_ref, other_ref, row_ref, out_ref):
    other = other_ref[0].astype(F32)
    row = row_ref[0:1] + (other[20:21] + other[21:22] + other[22:23])
    terms = jnp.concatenate([jnp.zeros((20, LANES), F32), split_row(row)], axis=0)
    is_right = lax.broadcasted_iota(jnp.int32, (1, CHUNK, LANES), 1) < 20
    for start in range(0, CHIPS, 8):
        both = own_ref[start : start + 8] + other_ref[start : start + 8].astype(F32)
        out_ref[start : start + 8] = jnp.where(is_right, both, terms[None]).astype(BF16)


def inverse_factors(grams):
    row = lax.broadcasted_iota(jnp.int32, (RANK, LANES), 0)
    lane = lax.broadcasted_iota(jnp.int32, (RANK, LANES), 1)
    first = (lane // RANK) % 2 == 0
    eye = (lane % RANK == row).astype(F32)
    square = jnp.concatenate(list(grams) + [jnp.zeros((RANK, LANES - BOTH), F32)], axis=1)
    diagonal = square * eye
    trace = [
        jnp.sum(jnp.where(lane // RANK == m, diagonal, 0.0), axis=(0, 1), keepdims=True) for m in range(MATS)
    ]
    shift = 1e-05 * jnp.where(first, trace[0], trace[1]) / RANK
    work = square + jnp.where(lane < BOTH, shift * eye, eye)
    for start in range(0, RANK, BLOCK):
        columns = [jnp.where(first, work[:, j : j + 1], work[:, RANK + j : RANK + j + 1]) for j in range(start, start + BLOCK)]
        rows = [work[j : j + 1, :] for j in range(start, start + BLOCK)]
        update = jnp.zeros_like(work)
        for a in range(BLOCK):
            inverse_pivot = 1.0 / columns[a][start + a : start + a + 1, :]
            scaled = rows[a] * inverse_pivot
            below = jnp.where(row > start + a, columns[a], 0.0)
            update = update + below * scaled
            for b in range(a + 1, BLOCK):
                value = columns[a][start + b : start + b + 1, :]
                rows[b] = rows[b] - value * scaled
                columns[b] = columns[b] - below * (value * inverse_pivot)
        work = work - update
    pivots = work * eye
    pivot = [
        jnp.sum(jnp.where(lane // RANK == m, pivots, 0.0), axis=1, keepdims=True) for m in range(MATS)
    ]
    return work / jnp.sqrt(jnp.where(first, pivot[0], pivot[1]))


def factor_kernel(parts_ref, summed_ref, out_ref, p_ref, left_ref, gram_ref):
    total = jnp.zeros((CHUNK, LANES), F32)
    for r in range(DP):
        places = [CHIP_ORDER.index(CHIPS_X * r + x) for x in range(CHIPS_X)]
        block = parts_ref[places[0]].astype(F32)
        for place in places[1:]:
            block = block + parts_ref[place].astype(F32)
        total = total + block
        gram_ref[r : r + 1, :] = block[20:21] + block[21:22] + block[22:23]
    gram = gram_ref[...]
    gram = jnp.concatenate([gram[:, RANK * a : RANK * a + RANK] for a in range(4)], axis=0)
    inverse = inverse_factors([gram[m * RANK : (m + 1) * RANK] for m in range(MATS)])

    lane = lax.broadcasted_iota(jnp.int32, (RANK, LANES), 1)
    turned = pltpu.roll(inverse, BOTH, 1)
    weights = jnp.concatenate(
        [
            jnp.where(lane // RANK == 2 * g + m, inverse if g else turned, 0.0)
            for g in range(2)
            for m in range(MATS)
        ],
        axis=0,
    )
    right = lax.dot_general(total, weights, NT, precision=HIGHEST, preferred_element_type=F32) / DP
    row = lax.broadcasted_iota(jnp.int32, (CHUNK, LANES), 0)
    right = jnp.where(row < 20, right, 0.0).astype(BF16)
    out_ref[...] = jnp.broadcast_to(right[None], out_ref.shape)
    p = lax.dot_general(
        weights[:BOTH, :BOTH], summed_ref[...], NN, precision=HIGHEST, preferred_element_type=F32
    )
    p_ref[...] = p
    p = p.T
    p = jnp.concatenate([p, p], axis=1)
    lane = lax.broadcasted_iota(jnp.int32, (ROWS, LANES), 1)
    for g in range(2):
        for m in range(MATS):
            left_ref[g, ROWS * m : ROWS * m + ROWS, :] = jnp.where(lane // RANK == 2 * g + m, p, 0.0).astype(BF16)


def piece_copy(stage, out_ref, core, piece, sem):
    g, first, size = piece
    columns = pl.ds(pl.multiple_of(HALF * core + QUARTER * g + first, LANES), size)
    return pltpu.make_async_copy(stage, out_ref.at[:, :, columns], sem)


def half_error(right_ref, left_ref, corrected_ref, out_ref, core, wide_ref, tail_ref, turned_ref, stage_ref, sems, rest_ref=None):
    for n in range(CHIPS // 16):
        block = right_ref[16 * n : 16 * n + 16].astype(F32)
        wide_ref[256 * n : 256 * n + 256, :] = block[:, 0:16].reshape(256, LANES)
        tail_ref[128 * n : 128 * n + 128, :] = block[:, 16:24].reshape(128, LANES)
    for n in range(4):
        wide_ref[HEAD + CHIPS * n : HEAD + CHIPS * n + CHIPS, :] = tail_ref[pl.ds(n, CHIPS, stride=8), :]
    turned_ref[...] = wide_ref[:QUARTER, :].astype(BF16)

    copies = []
    for n, (g, first, size) in enumerate(PIECES):
        columns = pl.ds(pl.multiple_of(HALF * core + QUARTER * g + first, LANES), size)
        rebuilt = lax.dot_general(
            left_ref[g], turned_ref[first : first + size, :], NT, preferred_element_type=F32
        )
        keep = rest_ref is not None and n == len(PIECES) - 1
        stage = rest_ref if keep else stage_ref.at[:, :, pl.ds(QUARTER * g + first, size)]
        for m in range(MATS):
            stage[m] = (
                corrected_ref[m, :, columns].astype(F32) - rebuilt[ROWS * m : ROWS * m + ROWS]
            ).astype(BF16)
        if not keep:
            copies.append(piece_copy(stage, out_ref, core, PIECES[n], sems.at[n]))
            copies[-1].start()

    me = lax.axis_index("dp") * TENSOR + lax.axis_index("tensor")
    wide_ref[QUARTER:, :] = jnp.zeros((LANES, LANES), F32)
    start = pl.multiple_of(SHARE * (me % (DEVICES // 4)), 8)
    own = wide_ref[pl.ds(start, LANES), :].T
    upper = (me // (DEVICES // 4)) % 2 == 1
    return copies, jnp.where(upper, own[BOTH:, :SHARE], own[:BOTH, :SHARE])


def own_error_kernel(
    right_ref, left_ref, corrected_ref, p_ref, out_ref, q_ref, rest_ref, p_out_ref, *scratch
):
    *scratch, p_sem = scratch
    p_copy = pltpu.make_async_copy(p_ref, p_out_ref, p_sem)
    p_copy.start()
    core = lax.axis_index("tensor") % 2
    copies, q_ref[...] = half_error(right_ref, left_ref, corrected_ref, out_ref, core, *scratch, rest_ref)
    for copy in [*copies, p_copy]:
        copy.wait()


def other_error_kernel(
    right_ref, left_ref, corrected_ref, q_own_ref, rest_ref, error_ref, out_ref, q_out_ref, *scratch
):
    del error_ref
    *scratch, q_ref, rest_sem, q_sem = scratch
    core = lax.axis_index("tensor") % 2
    rest_copy = piece_copy(rest_ref, out_ref, core, PIECES[-1], rest_sem)
    rest_copy.start()
    copies, other = half_error(right_ref, left_ref, corrected_ref, out_ref, 1 - core, *scratch)
    me = lax.axis_index("dp") * TENSOR + lax.axis_index("tensor")
    q_ref[...] = jnp.where(me // CHIPS == core, q_own_ref[...], other)
    q_copy = pltpu.make_async_copy(q_ref, q_out_ref, q_sem)
    q_copy.start()
    for copy in [rest_copy, *copies, q_copy]:
        copy.wait()


WHOLE = pl.BlockSpec(memory_space=pltpu.VMEM)
IN_HBM = pl.BlockSpec(memory_space=pltpu.HBM)


def call(kernel, name, in_specs, out_shape, out_specs=None, scratch=(), flops=0, **extra):
    return pl.pallas_call(
        kernel,
        in_specs=in_specs,
        out_specs=out_specs or [WHOLE] * len(out_shape),
        out_shape=out_shape,
        scratch_shapes=list(scratch),
        compiler_params=pltpu.CompilerParams(vmem_limit_bytes=VMEM_BYTES),
        cost_estimate=pl.CostEstimate(flops=flops, bytes_accessed=4 << 20, transcendentals=0),
        name=name,
        **extra,
    )


def in_hbm(x):
    return pltpu.with_memory_space_constraint(x, pltpu.HBM)


def local(grad, error, q_init):
    corrected, part = call(
        left_kernel,
        "left_product",
        [IN_HBM] * 3,
        [pltpu.VMEM((MATS, ROWS, WIDTH), BF16), pltpu.VMEM((DP, BOTH, ROWS), BF16)],
        scratch=[
            pltpu.VMEM((MATS, ROWS, WIDTH), BF16),
            pltpu.VMEM((MATS, RANK, WIDTH), BF16),
            pltpu.VMEM((MATS, ROWS, RANK), F32),
            pltpu.SemaphoreType.DMA((3, len(READS))),
        ],
    )(in_hbm(grad[0]), in_hbm(error[0]), in_hbm(q_init.transpose(1, 2, 0)))

    parts = lax.all_to_all(part, "dp", 0, 0, axis_index_groups=[DP_ORDER], tiled=True)

    turned = pltpu.VMEM((QUARTER, LANES), F32)
    tail = pltpu.VMEM((CHIPS * 8, LANES), F32)
    chunks = pltpu.VMEM((CHIPS, CHUNK, LANES), BF16)
    half_flops = 2 * MATS * ROWS * HALF * RANK
    for_other, summed, gram_row = call(
        other_half_kernel,
        "right_product_other",
        [WHOLE] * 2,
        [chunks, pltpu.VMEM((BOTH, ROWS), F32), pltpu.VMEM((8, LANES), F32)],
        scratch=[turned, tail, pltpu.VMEM((16, LANES), F32)],
        flops=half_flops,
    )(parts, corrected)
    from_other = lax.ppermute(for_other, "tensor", CORE_PAIRS)
    own = call(
        own_half_kernel,
        "right_product_own",
        [WHOLE] * 2,
        [pltpu.VMEM((CHIPS, CHUNK, LANES), F32)],
        scratch=[turned, tail],
        flops=half_flops,
    )(summed, corrected)[0]
    partial_q = call(pair_sum_kernel, "pair_sum", [WHOLE] * 3, [chunks])(own, from_other, gram_row)[0]

    partial_q = lax.all_to_all(partial_q, BOTH_AXES, 0, 0, axis_index_groups=SAME_CORE, tiled=True)

    q_own, p_turned, left = call(
        factor_kernel,
        "factor",
        [WHOLE] * 2,
        [chunks, pltpu.VMEM((BOTH, ROWS), F32), pltpu.VMEM((2, MATS * ROWS, LANES), BF16)],
        scratch=[pltpu.VMEM((16, LANES), F32)],
    )(partial_q, summed)

    q_half = lax.all_to_all(q_own, BOTH_AXES, 0, 0, axis_index_groups=SAME_CORE, tiled=True)

    q_other = lax.ppermute(q_half, "tensor", CORE_PAIRS)
    scratch = [
        pltpu.VMEM((QUARTER + LANES, LANES), F32),
        tail,
        pltpu.VMEM((QUARTER, LANES), BF16),
        pltpu.VMEM((MATS, ROWS, HALF), BF16),
        pltpu.SemaphoreType.DMA((len(PIECES),)),
    ]
    error_shape = jax.ShapeDtypeStruct((MATS, ROWS, WIDTH), BF16)
    factor_shape = jax.ShapeDtypeStruct((BOTH, ROWS), F32)
    rest_shape = pltpu.VMEM((MATS, ROWS, PIECES[-1][2]), BF16)
    new_error, q_factor, rest, p_factor = call(
        own_error_kernel,
        "new_error_own",
        [WHOLE] * 4,
        [error_shape, pltpu.VMEM((BOTH, SHARE), F32), rest_shape, factor_shape],
        [IN_HBM, WHOLE, WHOLE, IN_HBM],
        scratch=[*scratch, pltpu.SemaphoreType.DMA],
        flops=half_flops,
    )(q_half, left, corrected, p_turned)
    new_error, q_factor = call(
        other_error_kernel,
        "new_error_other",
        [WHOLE] * 5 + [IN_HBM],
        [error_shape, jax.ShapeDtypeStruct((BOTH, SHARE), F32)],
        [IN_HBM, IN_HBM],
        scratch=[*scratch, pltpu.VMEM((BOTH, SHARE), F32), pltpu.SemaphoreType.DMA, pltpu.SemaphoreType.DMA],
        flops=half_flops,
        input_output_aliases={5: 0},
    )(q_other, left, corrected, q_factor, rest, new_error)

    return (
        new_error[None],
        p_factor.reshape(MATS, RANK, ROWS).transpose(0, 2, 1),
        q_factor.reshape(MATS, RANK, SHARE).transpose(2, 0, 1),
    )


def solution(mesh):
    in_specs = (P("dp", None, "tensor", None), P("dp", None, "tensor", None), P())
    out_specs = (
        P("dp", None, "tensor", None),
        P(None, "tensor", None),
        P(("dp", "tensor"), None, None),
    )
    return jax.shard_map(local, mesh=mesh, in_specs=in_specs, out_specs=out_specs, check_vma=False)
```

```python
import functools

import jax
import jax.numpy as jnp
from jax import lax
from jax.experimental import pallas as pl
from jax.experimental.pallas import tpu as pltpu
from jax.sharding import PartitionSpec as P

F32 = jnp.float32
BF16 = jnp.bfloat16
HIGHEST = lax.Precision.HIGHEST
NN = (((1,), (0,)), ((), ()))
NT = (((1,), (1,)), ((), ()))
VMEM_BYTES = 36 * 1024 * 1024

MATS, ROWS, WIDTH, RANK = 2, 384, 5120, 32
BOTH = MATS * RANK
HALF, QUARTER = WIDTH // 2, WIDTH // 4
LANES = 2 * BOTH
DP, TENSOR = 16, 8
DEVICES = DP * TENSOR
CHIPS = DEVICES // 2
CHIPS_X = TENSOR // 2
SHARE = WIDTH // DEVICES
HEAD = 16 * CHIPS
CHUNK = 24
READS = [1280, 1280, 1280, 768, 512]
TILE = 256
BLOCK = 16
PIECES = [(0, 0, 640), (0, 640, 640), (1, 0, 640), (1, 640, 640)]
DP_ORDER = [10, 0, 14, 13, 7, 1, 2, 3, 15, 9, 12, 6, 8, 11, 5, 4]
CHIP_ORDER = [
    42, 52, 40, 44, 60, 63, 24, 54, 0, 11, 45, 56, 18, 34, 10, 55,
    46, 38, 15, 31, 57, 61, 36, 5, 17, 62, 21, 22, 49, 6, 1, 29,
    41, 33, 28, 30, 51, 8, 2, 26, 32, 48, 7, 27, 23, 25, 4, 39,
    37, 14, 59, 19, 43, 16, 47, 20, 3, 53, 13, 50, 35, 9, 12, 58,
]
BOTH_AXES = ("dp", "tensor")
CORE_PAIRS = [(i, i ^ 1) for i in range(TENSOR)]
SAME_CORE = [[2 * chip + core for chip in CHIP_ORDER] for core in range(2)]


def columns_at(start, size):
    return pl.ds(pl.multiple_of(start, TILE), size)


def left_kernel(grad_ref, error_ref, q_ref, corrected_ref, out_ref, error_vmem, q_vmem, acc_ref, sems):
    reads = [pl.ds(sum(READS[:i]), size) for i, size in enumerate(READS)]
    copies = []
    for i, columns in enumerate(reads):
        pairs = [(q_ref, q_vmem), (grad_ref, corrected_ref), (error_ref, error_vmem)]
        copies.append(
            [
                pltpu.make_async_copy(source.at[:, :, columns], target.at[:, :, columns], sems.at[n, i])
                for n, (source, target) in enumerate(pairs)
            ]
        )
        for copy in copies[-1]:
            copy.start()
    for i, columns in enumerate(reads):
        for copy in copies[i]:
            copy.wait()
        for m in range(MATS):
            corrected = (corrected_ref[m, :, columns].astype(F32) + error_vmem[m, :, columns].astype(F32)).astype(BF16)
            corrected_ref[m, :, columns] = corrected
            product = lax.dot_general(corrected, q_vmem[m, :, columns], NT, preferred_element_type=F32)
            if i == 0:
                acc_ref[m] = product
            else:
                acc_ref[m] += product
    part = jnp.concatenate([acc_ref[m].T for m in range(MATS)], axis=0).astype(BF16)
    for r in range(DP):
        out_ref[r] = part


def split_row(row):
    high = row.astype(BF16).astype(F32)
    middle = (row - high).astype(BF16).astype(F32)
    low = row - high - middle
    return jnp.concatenate([high, middle, low, jnp.zeros_like(row)], axis=0)


def half_product(left, corrected_ref, core, turned_ref):
    def columns_step(i, carry):
        products = []
        for g in range(2):
            columns = columns_at(HALF * core + QUARTER * g + TILE * i, TILE)
            for m in range(MATS):
                products.append(
                    lax.dot_general(left[m], corrected_ref[m, :, columns], NN, preferred_element_type=F32)
                )
        turned_ref[columns_at(TILE * i, TILE), :] = jnp.concatenate(products, axis=0).T
        return carry

    lax.fori_loop(0, QUARTER // TILE, columns_step, 0, unroll=True)


def chunked(turned_ref, tail_ref, terms):
    for n in range(4):
        tail_ref[pl.ds(n, CHIPS, stride=8), :] = turned_ref[HEAD + CHIPS * n : HEAD + CHIPS * n + CHIPS, :]
        tail_ref[pl.ds(n + 4, CHIPS, stride=8), :] = jnp.broadcast_to(terms[n : n + 1], (CHIPS, LANES))
    for n in range(CHIPS // 16):
        head = turned_ref[256 * n : 256 * n + 256, :].reshape(16, 16, LANES)
        tail = tail_ref[128 * n : 128 * n + 128, :].reshape(16, 8, LANES)
        yield 16 * n, jnp.concatenate([head, tail], axis=1)


def other_half_kernel(
    parts_ref, corrected_ref, out_ref, summed_ref, row_ref, turned_ref, tail_ref, gram_ref
):
    summed = parts_ref[0].astype(F32)
    for r in range(1, DP):
        summed = summed + parts_ref[r].astype(F32)
    summed_ref[...] = summed
    left = [summed[m * RANK : (m + 1) * RANK] for m in range(MATS)]
    core = lax.axis_index("tensor") % 2
    half_product([x.astype(BF16) for x in left], corrected_ref, 1 - core, turned_ref)

    gram = jnp.concatenate(
        [lax.dot_general(x, x, NT, precision=HIGHEST, preferred_element_type=F32) for x in left], axis=0
    )
    gram_ref[...] = jnp.concatenate([gram[16 * a : 16 * a + 16] for a in range(4)], axis=1)
    row = gram_ref[pl.ds(lax.axis_index("dp"), 1), :]
    row_ref[...] = jnp.broadcast_to(row, row_ref.shape)
    for start, chunks in chunked(turned_ref, tail_ref, split_row(row)):
        out_ref[start : start + 16] = chunks.astype(BF16)


def own_half_kernel(summed_ref, corrected_ref, out_ref, turned_ref, tail_ref):
    left = [summed_ref[m * RANK : (m + 1) * RANK].astype(BF16) for m in range(MATS)]
    half_product(left, corrected_ref, lax.axis_index("tensor") % 2, turned_ref)
    for start, chunks in chunked(turned_ref, tail_ref, jnp.zeros((4, LANES), F32)):
        out_ref[start : start + 16] = chunks


def pair_sum_kernel(own_ref, other_ref, row_ref, out_ref):
    other = other_ref[0].astype(F32)
    row = row_ref[0:1] + (other[20:21] + other[21:22] + other[22:23])
    terms = jnp.concatenate([jnp.zeros((20, LANES), F32), split_row(row)], axis=0)
    is_right = lax.broadcasted_iota(jnp.int32, (1, CHUNK, LANES), 1) < 20
    for start in range(0, CHIPS, 8):
        both = own_ref[start : start + 8] + other_ref[start : start + 8].astype(F32)
        out_ref[start : start + 8] = jnp.where(is_right, both, terms[None]).astype(BF16)


def inverse_factors(grams):
    row = lax.broadcasted_iota(jnp.int32, (RANK, LANES), 0)
    lane = lax.broadcasted_iota(jnp.int32, (RANK, LANES), 1)
    first = (lane // RANK) % 2 == 0
    eye = (lane % RANK == row).astype(F32)
    square = jnp.concatenate(list(grams) + [jnp.zeros((RANK, LANES - BOTH), F32)], axis=1)
    diagonal = square * eye
    trace = [
        jnp.sum(jnp.where(lane // RANK == m, diagonal, 0.0), axis=(0, 1), keepdims=True) for m in range(MATS)
    ]
    shift = 1e-05 * jnp.where(first, trace[0], trace[1]) / RANK
    work = square + jnp.where(lane < BOTH, shift * eye, eye)
    for start in range(0, RANK, BLOCK):
        columns = [jnp.where(first, work[:, j : j + 1], work[:, RANK + j : RANK + j + 1]) for j in range(start, start + BLOCK)]
        rows = [work[j : j + 1, :] for j in range(start, start + BLOCK)]
        update = jnp.zeros_like(work)
        for a in range(BLOCK):
            inverse_pivot = 1.0 / columns[a][start + a : start + a + 1, :]
            scaled = rows[a] * inverse_pivot
            below = jnp.where(row > start + a, columns[a], 0.0)
            update = update + below * scaled
            for b in range(a + 1, BLOCK):
                value = columns[a][start + b : start + b + 1, :]
                rows[b] = rows[b] - value * scaled
                columns[b] = columns[b] - below * (value * inverse_pivot)
        work = work - update
    pivots = work * eye
    pivot = [
        jnp.sum(jnp.where(lane // RANK == m, pivots, 0.0), axis=1, keepdims=True) for m in range(MATS)
    ]
    return work / jnp.sqrt(jnp.where(first, pivot[0], pivot[1]))


def factor_kernel(parts_ref, summed_ref, out_ref, p_ref, left_ref, gram_ref):
    total = jnp.zeros((CHUNK, LANES), F32)
    for r in range(DP):
        places = [CHIP_ORDER.index(CHIPS_X * r + x) for x in range(CHIPS_X)]
        block = parts_ref[places[0]].astype(F32)
        for place in places[1:]:
            block = block + parts_ref[place].astype(F32)
        total = total + block
        gram_ref[r : r + 1, :] = block[20:21] + block[21:22] + block[22:23]
    gram = gram_ref[...]
    gram = jnp.concatenate([gram[:, RANK * a : RANK * a + RANK] for a in range(4)], axis=0)
    inverse = inverse_factors([gram[m * RANK : (m + 1) * RANK] for m in range(MATS)])

    lane = lax.broadcasted_iota(jnp.int32, (RANK, LANES), 1)
    turned = pltpu.roll(inverse, BOTH, 1)
    weights = jnp.concatenate(
        [
            jnp.where(lane // RANK == 2 * g + m, inverse if g else turned, 0.0)
            for g in range(2)
            for m in range(MATS)
        ],
        axis=0,
    )
    right = lax.dot_general(total, weights, NT, precision=HIGHEST, preferred_element_type=F32) / DP
    row = lax.broadcasted_iota(jnp.int32, (CHUNK, LANES), 0)
    right = jnp.where(row < 20, right, 0.0).astype(BF16)
    out_ref[...] = jnp.broadcast_to(right[None], out_ref.shape)
    p = lax.dot_general(
        weights[:BOTH, :BOTH], summed_ref[...], NN, precision=HIGHEST, preferred_element_type=F32
    )
    p_ref[...] = p
    p = p.T
    p = jnp.concatenate([p, p], axis=1)
    lane = lax.broadcasted_iota(jnp.int32, (ROWS, LANES), 1)
    for g in range(2):
        for m in range(MATS):
            left_ref[g, ROWS * m : ROWS * m + ROWS, :] = jnp.where(lane // RANK == 2 * g + m, p, 0.0).astype(BF16)


def piece_copy(stage, out_ref, core, piece, sem):
    g, first, size = piece
    columns = pl.ds(pl.multiple_of(HALF * core + QUARTER * g + first, LANES), size)
    return pltpu.make_async_copy(stage, out_ref.at[:, :, columns], sem)


def half_error(right_ref, left_ref, corrected_ref, out_ref, core, wide_ref, tail_ref, turned_ref, stage_ref, sems, rest_ref=None):
    for n in range(CHIPS // 16):
        block = right_ref[16 * n : 16 * n + 16].astype(F32)
        wide_ref[256 * n : 256 * n + 256, :] = block[:, 0:16].reshape(256, LANES)
        tail_ref[128 * n : 128 * n + 128, :] = block[:, 16:24].reshape(128, LANES)
    for n in range(4):
        wide_ref[HEAD + CHIPS * n : HEAD + CHIPS * n + CHIPS, :] = tail_ref[pl.ds(n, CHIPS, stride=8), :]
    turned_ref[...] = wide_ref[:QUARTER, :].astype(BF16)

    copies = []
    for n, (g, first, size) in enumerate(PIECES):
        columns = pl.ds(pl.multiple_of(HALF * core + QUARTER * g + first, LANES), size)
        rebuilt = lax.dot_general(
            left_ref[g], turned_ref[first : first + size, :], NT, preferred_element_type=F32
        )
        keep = rest_ref is not None and n == len(PIECES) - 1
        stage = rest_ref if keep else stage_ref.at[:, :, pl.ds(QUARTER * g + first, size)]
        for m in range(MATS):
            stage[m] = (
                corrected_ref[m, :, columns].astype(F32) - rebuilt[ROWS * m : ROWS * m + ROWS]
            ).astype(BF16)
        if not keep:
            copies.append(piece_copy(stage, out_ref, core, PIECES[n], sems.at[n]))
            copies[-1].start()

    me = lax.axis_index("dp") * TENSOR + lax.axis_index("tensor")
    wide_ref[QUARTER:, :] = jnp.zeros((LANES, LANES), F32)
    start = pl.multiple_of(SHARE * (me % (DEVICES // 4)), 8)
    own = wide_ref[pl.ds(start, LANES), :].T
    upper = (me // (DEVICES // 4)) % 2 == 1
    return copies, jnp.where(upper, own[BOTH:, :SHARE], own[:BOTH, :SHARE])


def own_error_kernel(turn, right_ref, left_ref, corrected_ref, *refs):
    out_ref, q_ref, rest_ref, *scratch = refs[turn_inputs(turn) :]
    core = lax.axis_index("tensor") % 2

    @pl.when(core == turn)
    def _():
        copies, q_ref[...] = half_error(right_ref, left_ref, corrected_ref, out_ref, core, *scratch, rest_ref)
        for copy in copies:
            copy.wait()


def turn_inputs(turn):
    return 1 if turn == 0 else 0


def other_error_kernel(
    right_ref, left_ref, corrected_ref, q_0_ref, rest_0_ref, q_1_ref, rest_1_ref, p_ref, error_ref,
    out_ref, q_out_ref, p_out_ref, *scratch,
):
    del error_ref
    *scratch, q_ref, rest_sem, q_sem, p_sem = scratch
    core = lax.axis_index("tensor") % 2
    p_copy = pltpu.make_async_copy(p_ref, p_out_ref, p_sem)
    p_copy.start()
    rest_copies = [piece_copy(rest, out_ref, core, PIECES[-1], rest_sem) for rest in (rest_0_ref, rest_1_ref)]
    for turn, copy in enumerate(rest_copies):
        pl.when(core == turn)(copy.start)
    copies, other = half_error(right_ref, left_ref, corrected_ref, out_ref, 1 - core, *scratch)
    me = lax.axis_index("dp") * TENSOR + lax.axis_index("tensor")
    own = jnp.where(core == 0, q_0_ref[...], q_1_ref[...])
    q_ref[...] = jnp.where(me // CHIPS == core, own, other)
    q_copy = pltpu.make_async_copy(q_ref, q_out_ref, q_sem)
    q_copy.start()
    for copy in [*copies, q_copy, p_copy]:
        copy.wait()
    for turn, copy in enumerate(rest_copies):
        pl.when(core == turn)(copy.wait)


WHOLE = pl.BlockSpec(memory_space=pltpu.VMEM)
IN_HBM = pl.BlockSpec(memory_space=pltpu.HBM)


def call(kernel, name, in_specs, out_shape, out_specs=None, scratch=(), flops=0, **extra):
    return pl.pallas_call(
        kernel,
        in_specs=in_specs,
        out_specs=out_specs or [WHOLE] * len(out_shape),
        out_shape=out_shape,
        scratch_shapes=list(scratch),
        compiler_params=pltpu.CompilerParams(vmem_limit_bytes=VMEM_BYTES),
        cost_estimate=pl.CostEstimate(flops=flops, bytes_accessed=4 << 20, transcendentals=0),
        name=name,
        **extra,
    )


def in_hbm(x):
    return pltpu.with_memory_space_constraint(x, pltpu.HBM)


def local(grad, error, q_init):
    corrected, part = call(
        left_kernel,
        "left_product",
        [IN_HBM] * 3,
        [pltpu.VMEM((MATS, ROWS, WIDTH), BF16), pltpu.VMEM((DP, BOTH, ROWS), BF16)],
        scratch=[
            pltpu.VMEM((MATS, ROWS, WIDTH), BF16),
            pltpu.VMEM((MATS, RANK, WIDTH), BF16),
            pltpu.VMEM((MATS, ROWS, RANK), F32),
            pltpu.SemaphoreType.DMA((3, len(READS))),
        ],
    )(in_hbm(grad[0]), in_hbm(error[0]), in_hbm(q_init.transpose(1, 2, 0)))

    parts = lax.all_to_all(part, "dp", 0, 0, axis_index_groups=[DP_ORDER], tiled=True)

    turned = pltpu.VMEM((QUARTER, LANES), F32)
    tail = pltpu.VMEM((CHIPS * 8, LANES), F32)
    chunks = pltpu.VMEM((CHIPS, CHUNK, LANES), BF16)
    half_flops = 2 * MATS * ROWS * HALF * RANK
    for_other, summed, gram_row = call(
        other_half_kernel,
        "right_product_other",
        [WHOLE] * 2,
        [chunks, pltpu.VMEM((BOTH, ROWS), F32), pltpu.VMEM((8, LANES), F32)],
        scratch=[turned, tail, pltpu.VMEM((16, LANES), F32)],
        flops=half_flops,
    )(parts, corrected)
    from_other = lax.ppermute(for_other, "tensor", CORE_PAIRS)
    own = call(
        own_half_kernel,
        "right_product_own",
        [WHOLE] * 2,
        [pltpu.VMEM((CHIPS, CHUNK, LANES), F32)],
        scratch=[turned, tail],
        flops=half_flops,
    )(summed, corrected)[0]
    partial_q = call(pair_sum_kernel, "pair_sum", [WHOLE] * 3, [chunks])(own, from_other, gram_row)[0]

    partial_q = lax.all_to_all(partial_q, BOTH_AXES, 0, 0, axis_index_groups=SAME_CORE, tiled=True)

    q_own, p_turned, left = call(
        factor_kernel,
        "factor",
        [WHOLE] * 2,
        [chunks, pltpu.VMEM((BOTH, ROWS), F32), pltpu.VMEM((2, MATS * ROWS, LANES), BF16)],
        scratch=[pltpu.VMEM((16, LANES), F32)],
    )(partial_q, summed)

    q_half = lax.all_to_all(q_own, BOTH_AXES, 0, 0, axis_index_groups=SAME_CORE, tiled=True)

    scratch = [
        pltpu.VMEM((QUARTER + LANES, LANES), F32),
        tail,
        pltpu.VMEM((QUARTER, LANES), BF16),
        pltpu.VMEM((MATS, ROWS, HALF), BF16),
        pltpu.SemaphoreType.DMA((len(PIECES),)),
    ]
    error_shape = jax.ShapeDtypeStruct((MATS, ROWS, WIDTH), BF16)
    factor_shape = jax.ShapeDtypeStruct((BOTH, ROWS), F32)
    rest_shape = pltpu.VMEM((MATS, ROWS, PIECES[-1][2]), BF16)
    own_shapes = [error_shape, pltpu.VMEM((BOTH, SHARE), F32), rest_shape]
    new_error, q_1, rest_1 = call(
        functools.partial(own_error_kernel, 1),
        "new_error_own_1",
        [WHOLE] * 3,
        own_shapes,
        [IN_HBM, WHOLE, WHOLE],
        scratch=scratch,
    )(q_half, left, corrected)
    q_half, new_error = lax.optimization_barrier((q_half, new_error))
    q_other = lax.ppermute(q_half, "tensor", CORE_PAIRS)
    new_error, q_0, rest_0 = call(
        functools.partial(own_error_kernel, 0),
        "new_error_own_0",
        [WHOLE] * 3 + [IN_HBM],
        own_shapes,
        [IN_HBM, WHOLE, WHOLE],
        scratch=scratch,
        flops=half_flops,
        input_output_aliases={3: 0},
    )(q_half, left, corrected, new_error)
    new_error, q_factor, p_factor = call(
        other_error_kernel,
        "new_error_other",
        [WHOLE] * 8 + [IN_HBM],
        [error_shape, jax.ShapeDtypeStruct((BOTH, SHARE), F32), factor_shape],
        [IN_HBM] * 3,
        scratch=[*scratch, pltpu.VMEM((BOTH, SHARE), F32)] + [pltpu.SemaphoreType.DMA] * 3,
        flops=half_flops,
        input_output_aliases={8: 0},
    )(q_other, left, corrected, q_0, rest_0, q_1, rest_1, p_turned, new_error)

    return (
        new_error[None],
        p_factor.reshape(MATS, RANK, ROWS).transpose(0, 2, 1),
        q_factor.reshape(MATS, RANK, SHARE).transpose(2, 0, 1),
    )


def solution(mesh):
    in_specs = (P("dp", None, "tensor", None), P("dp", None, "tensor", None), P())
    out_specs = (
        P("dp", None, "tensor", None),
        P(None, "tensor", None),
        P(("dp", "tensor"), None, None),
    )
    return jax.shard_map(local, mesh=mesh, in_specs=in_specs, out_specs=out_specs, check_vma=False)
```

```python
import functools

import jax
import jax.numpy as jnp
from jax import lax
from jax.experimental import pallas as pl
from jax.experimental.pallas import tpu as pltpu
from jax.sharding import PartitionSpec as P

F32 = jnp.float32
BF16 = jnp.bfloat16
HIGHEST = lax.Precision.HIGHEST
NN = (((1,), (0,)), ((), ()))
NT = (((1,), (1,)), ((), ()))
VMEM_BYTES = 36 * 1024 * 1024

MATS, ROWS, WIDTH, RANK = 2, 384, 5120, 32
BOTH = MATS * RANK
HALF, QUARTER = WIDTH // 2, WIDTH // 4
LANES = 2 * BOTH
DP, TENSOR = 16, 8
DEVICES = DP * TENSOR
CHIPS = DEVICES // 2
CHIPS_X = TENSOR // 2
SHARE = WIDTH // DEVICES
HEAD = 16 * CHIPS
CHUNK = 24
READS = [1280, 1280, 1280, 768, 512]
TILE = 256
BLOCK = 16
PIECES = [(0, 0, 640), (0, 640, 640), (1, 0, 640), (1, 640, 640)]
DP_ORDER = [10, 14, 7, 5, 2, 6, 15, 4, 0, 3, 8, 11, 1, 13, 9, 12]
CHIP_ORDER = [
    42, 52, 40, 44, 60, 63, 24, 54, 0, 11, 45, 56, 18, 34, 10, 55,
    46, 38, 15, 31, 57, 61, 36, 5, 17, 62, 21, 22, 49, 6, 1, 29,
    41, 33, 28, 30, 51, 8, 2, 26, 32, 48, 7, 27, 23, 25, 4, 39,
    37, 14, 59, 19, 43, 16, 47, 20, 3, 53, 13, 50, 35, 9, 12, 58,
]
BOTH_AXES = ("dp", "tensor")
CORE_PAIRS = [(i, i ^ 1) for i in range(TENSOR)]
SAME_CORE = [[2 * chip + core for chip in CHIP_ORDER] for core in range(2)]


def columns_at(start, size):
    return pl.ds(pl.multiple_of(start, TILE), size)


def left_kernel(grad_ref, error_ref, q_ref, corrected_ref, out_ref, error_vmem, q_vmem, acc_ref, sems):
    reads = [pl.ds(sum(READS[:i]), size) for i, size in enumerate(READS)]
    copies = []
    for i, columns in enumerate(reads):
        pairs = [(q_ref, q_vmem), (grad_ref, corrected_ref), (error_ref, error_vmem)]
        copies.append(
            [
                pltpu.make_async_copy(source.at[:, :, columns], target.at[:, :, columns], sems.at[n, i])
                for n, (source, target) in enumerate(pairs)
            ]
        )
        for copy in copies[-1]:
            copy.start()
    for i, columns in enumerate(reads):
        for copy in copies[i]:
            copy.wait()
        for m in range(MATS):
            corrected = (corrected_ref[m, :, columns].astype(F32) + error_vmem[m, :, columns].astype(F32)).astype(BF16)
            corrected_ref[m, :, columns] = corrected
            product = lax.dot_general(corrected, q_vmem[m, :, columns], NT, preferred_element_type=F32)
            if i == 0:
                acc_ref[m] = product
            else:
                acc_ref[m] += product
    part = jnp.concatenate([acc_ref[m].T for m in range(MATS)], axis=0).astype(BF16)
    for r in range(DP):
        out_ref[r] = part


def split_row(row):
    high = row.astype(BF16).astype(F32)
    middle = (row - high).astype(BF16).astype(F32)
    low = row - high - middle
    return jnp.concatenate([high, middle, low, jnp.zeros_like(row)], axis=0)


def half_product(left, corrected_ref, core, turned_ref):
    def columns_step(i, carry):
        products = []
        for g in range(2):
            columns = columns_at(HALF * core + QUARTER * g + TILE * i, TILE)
            for m in range(MATS):
                products.append(
                    lax.dot_general(left[m], corrected_ref[m, :, columns], NN, preferred_element_type=F32)
                )
        turned_ref[columns_at(TILE * i, TILE), :] = jnp.concatenate(products, axis=0).T
        return carry

    lax.fori_loop(0, QUARTER // TILE, columns_step, 0, unroll=True)


def chunked(turned_ref, tail_ref, terms):
    for n in range(4):
        tail_ref[pl.ds(n, CHIPS, stride=8), :] = turned_ref[HEAD + CHIPS * n : HEAD + CHIPS * n + CHIPS, :]
        tail_ref[pl.ds(n + 4, CHIPS, stride=8), :] = jnp.broadcast_to(terms[n : n + 1], (CHIPS, LANES))
    for n in range(CHIPS // 16):
        head = turned_ref[256 * n : 256 * n + 256, :].reshape(16, 16, LANES)
        tail = tail_ref[128 * n : 128 * n + 128, :].reshape(16, 8, LANES)
        yield 16 * n, jnp.concatenate([head, tail], axis=1)


def other_half_kernel(
    parts_ref, corrected_ref, out_ref, summed_ref, row_ref, turned_ref, tail_ref, gram_ref
):
    summed = parts_ref[0].astype(F32)
    for r in range(1, DP):
        summed = summed + parts_ref[r].astype(F32)
    summed_ref[...] = summed
    left = [summed[m * RANK : (m + 1) * RANK] for m in range(MATS)]
    core = lax.axis_index("tensor") % 2
    half_product([x.astype(BF16) for x in left], corrected_ref, 1 - core, turned_ref)

    gram = jnp.concatenate(
        [lax.dot_general(x, x, NT, precision=HIGHEST, preferred_element_type=F32) for x in left], axis=0
    )
    gram_ref[...] = jnp.concatenate([gram[16 * a : 16 * a + 16] for a in range(4)], axis=1)
    row = gram_ref[pl.ds(lax.axis_index("dp"), 1), :]
    row_ref[...] = jnp.broadcast_to(row, row_ref.shape)
    for start, chunks in chunked(turned_ref, tail_ref, split_row(row)):
        out_ref[start : start + 16] = chunks.astype(BF16)


def own_half_kernel(summed_ref, corrected_ref, out_ref, turned_ref, tail_ref):
    left = [summed_ref[m * RANK : (m + 1) * RANK].astype(BF16) for m in range(MATS)]
    half_product(left, corrected_ref, lax.axis_index("tensor") % 2, turned_ref)
    for start, chunks in chunked(turned_ref, tail_ref, jnp.zeros((4, LANES), F32)):
        out_ref[start : start + 16] = chunks


def pair_sum_kernel(own_ref, other_ref, row_ref, out_ref):
    other = other_ref[0].astype(F32)
    row = row_ref[0:1] + (other[20:21] + other[21:22] + other[22:23])
    terms = jnp.concatenate([jnp.zeros((20, LANES), F32), split_row(row)], axis=0)
    is_right = lax.broadcasted_iota(jnp.int32, (1, CHUNK, LANES), 1) < 20
    for start in range(0, CHIPS, 8):
        both = own_ref[start : start + 8] + other_ref[start : start + 8].astype(F32)
        out_ref[start : start + 8] = jnp.where(is_right, both, terms[None]).astype(BF16)


def inverse_factors(grams):
    row = lax.broadcasted_iota(jnp.int32, (RANK, LANES), 0)
    lane = lax.broadcasted_iota(jnp.int32, (RANK, LANES), 1)
    first = (lane // RANK) % 2 == 0
    eye = (lane % RANK == row).astype(F32)
    square = jnp.concatenate(list(grams) + [jnp.zeros((RANK, LANES - BOTH), F32)], axis=1)
    diagonal = square * eye
    trace = [
        jnp.sum(jnp.where(lane // RANK == m, diagonal, 0.0), axis=(0, 1), keepdims=True) for m in range(MATS)
    ]
    shift = 1e-05 * jnp.where(first, trace[0], trace[1]) / RANK
    work = square + jnp.where(lane < BOTH, shift * eye, eye)
    for start in range(0, RANK, BLOCK):
        columns = [jnp.where(first, work[:, j : j + 1], work[:, RANK + j : RANK + j + 1]) for j in range(start, start + BLOCK)]
        rows = [work[j : j + 1, :] for j in range(start, start + BLOCK)]
        update = jnp.zeros_like(work)
        for a in range(BLOCK):
            inverse_pivot = 1.0 / columns[a][start + a : start + a + 1, :]
            scaled = rows[a] * inverse_pivot
            below = jnp.where(row > start + a, columns[a], 0.0)
            update = update + below * scaled
            for b in range(a + 1, BLOCK):
                value = columns[a][start + b : start + b + 1, :]
                rows[b] = rows[b] - value * scaled
                columns[b] = columns[b] - below * (value * inverse_pivot)
        work = work - update
    pivots = work * eye
    pivot = [
        jnp.sum(jnp.where(lane // RANK == m, pivots, 0.0), axis=1, keepdims=True) for m in range(MATS)
    ]
    return work / jnp.sqrt(jnp.where(first, pivot[0], pivot[1]))


def factor_kernel(parts_ref, summed_ref, out_ref, p_ref, left_ref, gram_ref):
    total = jnp.zeros((CHUNK, LANES), F32)
    for r in range(DP):
        places = [CHIP_ORDER.index(CHIPS_X * r + x) for x in range(CHIPS_X)]
        block = parts_ref[places[0]].astype(F32)
        for place in places[1:]:
            block = block + parts_ref[place].astype(F32)
        total = total + block
        gram_ref[r : r + 1, :] = block[20:21] + block[21:22] + block[22:23]
    gram = gram_ref[...]
    gram = jnp.concatenate([gram[:, RANK * a : RANK * a + RANK] for a in range(4)], axis=0)
    inverse = inverse_factors([gram[m * RANK : (m + 1) * RANK] for m in range(MATS)])

    lane = lax.broadcasted_iota(jnp.int32, (RANK, LANES), 1)
    turned = pltpu.roll(inverse, BOTH, 1)
    weights = jnp.concatenate(
        [
            jnp.where(lane // RANK == 2 * g + m, inverse if g else turned, 0.0)
            for g in range(2)
            for m in range(MATS)
        ],
        axis=0,
    )
    right = lax.dot_general(total, weights, NT, precision=HIGHEST, preferred_element_type=F32) / DP
    row = lax.broadcasted_iota(jnp.int32, (CHUNK, LANES), 0)
    right = jnp.where(row < 20, right, 0.0).astype(BF16)
    out_ref[...] = jnp.broadcast_to(right[None], out_ref.shape)
    p = lax.dot_general(
        weights[:BOTH, :BOTH], summed_ref[...], NN, precision=HIGHEST, preferred_element_type=F32
    )
    p_ref[...] = p
    p = p.T
    p = jnp.concatenate([p, p], axis=1)
    lane = lax.broadcasted_iota(jnp.int32, (ROWS, LANES), 1)
    for g in range(2):
        for m in range(MATS):
            left_ref[g, ROWS * m : ROWS * m + ROWS, :] = jnp.where(lane // RANK == 2 * g + m, p, 0.0).astype(BF16)


def piece_copy(stage, out_ref, core, piece, sem):
    g, first, size = piece
    columns = pl.ds(pl.multiple_of(HALF * core + QUARTER * g + first, LANES), size)
    return pltpu.make_async_copy(stage, out_ref.at[:, :, columns], sem)


def half_error(right_ref, left_ref, corrected_ref, out_ref, core, wide_ref, tail_ref, turned_ref, stage_ref, sems, rest_ref=None):
    for n in range(CHIPS // 16):
        block = right_ref[16 * n : 16 * n + 16].astype(F32)
        wide_ref[256 * n : 256 * n + 256, :] = block[:, 0:16].reshape(256, LANES)
        tail_ref[128 * n : 128 * n + 128, :] = block[:, 16:24].reshape(128, LANES)
    for n in range(4):
        wide_ref[HEAD + CHIPS * n : HEAD + CHIPS * n + CHIPS, :] = tail_ref[pl.ds(n, CHIPS, stride=8), :]
    turned_ref[...] = wide_ref[:QUARTER, :].astype(BF16)

    copies = []
    for n, (g, first, size) in enumerate(PIECES):
        columns = pl.ds(pl.multiple_of(HALF * core + QUARTER * g + first, LANES), size)
        rebuilt = lax.dot_general(
            left_ref[g], turned_ref[first : first + size, :], NT, preferred_element_type=F32
        )
        keep = rest_ref is not None and n == len(PIECES) - 1
        stage = rest_ref if keep else stage_ref.at[:, :, pl.ds(QUARTER * g + first, size)]
        for m in range(MATS):
            stage[m] = (
                corrected_ref[m, :, columns].astype(F32) - rebuilt[ROWS * m : ROWS * m + ROWS]
            ).astype(BF16)
        if not keep:
            copies.append(piece_copy(stage, out_ref, core, PIECES[n], sems.at[n]))
            copies[-1].start()

    me = lax.axis_index("dp") * TENSOR + lax.axis_index("tensor")
    wide_ref[QUARTER:, :] = jnp.zeros((LANES, LANES), F32)
    start = pl.multiple_of(SHARE * (me % (DEVICES // 4)), 8)
    own = wide_ref[pl.ds(start, LANES), :].T
    upper = (me // (DEVICES // 4)) % 2 == 1
    return copies, jnp.where(upper, own[BOTH:, :SHARE], own[:BOTH, :SHARE])


def own_error_kernel(turn, right_ref, left_ref, corrected_ref, *refs):
    out_ref, q_ref, rest_ref, *scratch = refs[turn_inputs(turn) :]
    core = lax.axis_index("tensor") % 2

    @pl.when(core == turn)
    def _():
        copies, q_ref[...] = half_error(right_ref, left_ref, corrected_ref, out_ref, core, *scratch, rest_ref)
        for copy in copies:
            copy.wait()


def turn_inputs(turn):
    return 1 if turn == 0 else 0


def other_error_kernel(
    right_ref, left_ref, corrected_ref, q_0_ref, rest_0_ref, q_1_ref, rest_1_ref, p_ref, error_ref,
    out_ref, q_out_ref, p_out_ref, *scratch,
):
    del error_ref
    *scratch, q_ref, rest_sem, q_sem, p_sem = scratch
    core = lax.axis_index("tensor") % 2
    p_copy = pltpu.make_async_copy(p_ref, p_out_ref, p_sem)
    p_copy.start()
    rest_copies = [piece_copy(rest, out_ref, core, PIECES[-1], rest_sem) for rest in (rest_0_ref, rest_1_ref)]
    for turn, copy in enumerate(rest_copies):
        pl.when(core == turn)(copy.start)
    copies, other = half_error(right_ref, left_ref, corrected_ref, out_ref, 1 - core, *scratch)
    me = lax.axis_index("dp") * TENSOR + lax.axis_index("tensor")
    own = jnp.where(core == 0, q_0_ref[...], q_1_ref[...])
    q_ref[...] = jnp.where(me // CHIPS == core, own, other)
    q_copy = pltpu.make_async_copy(q_ref, q_out_ref, q_sem)
    q_copy.start()
    for copy in [*copies, q_copy, p_copy]:
        copy.wait()
    for turn, copy in enumerate(rest_copies):
        pl.when(core == turn)(copy.wait)


WHOLE = pl.BlockSpec(memory_space=pltpu.VMEM)
IN_HBM = pl.BlockSpec(memory_space=pltpu.HBM)


def call(kernel, name, in_specs, out_shape, out_specs=None, scratch=(), flops=0, **extra):
    return pl.pallas_call(
        kernel,
        in_specs=in_specs,
        out_specs=out_specs or [WHOLE] * len(out_shape),
        out_shape=out_shape,
        scratch_shapes=list(scratch),
        compiler_params=pltpu.CompilerParams(vmem_limit_bytes=VMEM_BYTES),
        cost_estimate=pl.CostEstimate(flops=flops, bytes_accessed=4 << 20, transcendentals=0),
        name=name,
        **extra,
    )


def in_hbm(x):
    return pltpu.with_memory_space_constraint(x, pltpu.HBM)


def local(grad, error, q_init):
    corrected, part = call(
        left_kernel,
        "left_product",
        [IN_HBM] * 3,
        [pltpu.VMEM((MATS, ROWS, WIDTH), BF16), pltpu.VMEM((DP, BOTH, ROWS), BF16)],
        scratch=[
            pltpu.VMEM((MATS, ROWS, WIDTH), BF16),
            pltpu.VMEM((MATS, RANK, WIDTH), BF16),
            pltpu.VMEM((MATS, ROWS, RANK), F32),
            pltpu.SemaphoreType.DMA((3, len(READS))),
        ],
    )(in_hbm(grad[0]), in_hbm(error[0]), in_hbm(q_init.transpose(1, 2, 0)))

    parts = lax.all_to_all(part, "dp", 0, 0, axis_index_groups=[DP_ORDER], tiled=True)

    turned = pltpu.VMEM((QUARTER, LANES), F32)
    tail = pltpu.VMEM((CHIPS * 8, LANES), F32)
    chunks = pltpu.VMEM((CHIPS, CHUNK, LANES), BF16)
    half_flops = 2 * MATS * ROWS * HALF * RANK
    for_other, summed, gram_row = call(
        other_half_kernel,
        "right_product_other",
        [WHOLE] * 2,
        [chunks, pltpu.VMEM((BOTH, ROWS), F32), pltpu.VMEM((8, LANES), F32)],
        scratch=[turned, tail, pltpu.VMEM((16, LANES), F32)],
        flops=half_flops,
    )(parts, corrected)
    from_other = lax.ppermute(for_other, "tensor", CORE_PAIRS)
    own = call(
        own_half_kernel,
        "right_product_own",
        [WHOLE] * 2,
        [pltpu.VMEM((CHIPS, CHUNK, LANES), F32)],
        scratch=[turned, tail],
        flops=half_flops,
    )(summed, corrected)[0]
    partial_q = call(pair_sum_kernel, "pair_sum", [WHOLE] * 3, [chunks])(own, from_other, gram_row)[0]

    partial_q = lax.all_to_all(partial_q, BOTH_AXES, 0, 0, axis_index_groups=SAME_CORE, tiled=True)

    q_own, p_turned, left = call(
        factor_kernel,
        "factor",
        [WHOLE] * 2,
        [chunks, pltpu.VMEM((BOTH, ROWS), F32), pltpu.VMEM((2, MATS * ROWS, LANES), BF16)],
        scratch=[pltpu.VMEM((16, LANES), F32)],
    )(partial_q, summed)

    q_half = lax.all_to_all(q_own, BOTH_AXES, 0, 0, axis_index_groups=SAME_CORE, tiled=True)

    scratch = [
        pltpu.VMEM((QUARTER + LANES, LANES), F32),
        tail,
        pltpu.VMEM((QUARTER, LANES), BF16),
        pltpu.VMEM((MATS, ROWS, HALF), BF16),
        pltpu.SemaphoreType.DMA((len(PIECES),)),
    ]
    error_shape = jax.ShapeDtypeStruct((MATS, ROWS, WIDTH), BF16)
    factor_shape = jax.ShapeDtypeStruct((BOTH, ROWS), F32)
    rest_shape = pltpu.VMEM((MATS, ROWS, PIECES[-1][2]), BF16)
    own_shapes = [error_shape, pltpu.VMEM((BOTH, SHARE), F32), rest_shape]
    new_error, q_1, rest_1 = call(
        functools.partial(own_error_kernel, 1),
        "new_error_own_1",
        [WHOLE] * 3,
        own_shapes,
        [IN_HBM, WHOLE, WHOLE],
        scratch=scratch,
    )(q_half, left, corrected)
    q_half, new_error = lax.optimization_barrier((q_half, new_error))
    q_other = lax.ppermute(q_half, "tensor", CORE_PAIRS)
    new_error, q_0, rest_0 = call(
        functools.partial(own_error_kernel, 0),
        "new_error_own_0",
        [WHOLE] * 3 + [IN_HBM],
        own_shapes,
        [IN_HBM, WHOLE, WHOLE],
        scratch=scratch,
        flops=half_flops,
        input_output_aliases={3: 0},
    )(q_half, left, corrected, new_error)
    new_error, q_factor, p_factor = call(
        other_error_kernel,
        "new_error_other",
        [WHOLE] * 8 + [IN_HBM],
        [error_shape, jax.ShapeDtypeStruct((BOTH, SHARE), F32), factor_shape],
        [IN_HBM] * 3,
        scratch=[*scratch, pltpu.VMEM((BOTH, SHARE), F32)] + [pltpu.SemaphoreType.DMA] * 3,
        flops=half_flops,
        input_output_aliases={8: 0},
    )(q_other, left, corrected, q_0, rest_0, q_1, rest_1, p_turned, new_error)

    return (
        new_error[None],
        p_factor.reshape(MATS, RANK, ROWS).transpose(0, 2, 1),
        q_factor.reshape(MATS, RANK, SHARE).transpose(2, 0, 1),
    )


def solution(mesh):
    in_specs = (P("dp", None, "tensor", None), P("dp", None, "tensor", None), P())
    out_specs = (
        P("dp", None, "tensor", None),
        P(None, "tensor", None),
        P(("dp", "tensor"), None, None),
    )
    return jax.shard_map(local, mesh=mesh, in_specs=in_specs, out_specs=out_specs, check_vma=False)
```
